32 devices in a mesh: seq: 8 (over z, x), hap: 4 (over y, core).
Axes of the slice: x: 2, y: 2, z: 4, core: 2. Of those that a mesh axis runs over, the one named last changes fastest.
Arguments:
- tokens: bfloat16 [4, 1024, 512], P('hap', 'seq'), may hold values from -6 to 6
- cotangent: bfloat16 [4, 1024, 512], P('hap', 'seq'), may hold values from -6 to 6
- gaps: int32 [8, 2], P('seq'), may hold values from 0 to 128, as said below
- conv_taps: float32 [2, 3, 512], replicated, may hold values from -3.5 to 3.5
- norm_gains: float32 [2, 512], replicated, may hold values from 0.25 to 1.75
- projection: bfloat16 [2, 512, 1024], replicated, may hold values from -0.25 to 0.25
Outputs:
- tokens_grad: bfloat16 [4, 1024, 512], P('hap', 'seq')
- projection_grad: float32 [2, 512, 1024], P(None, 'seq')
- taps_grad: float32 [2, 3, 512], replicated
- gains_grad: float32 [2, 512], replicated
The draws below stay inside these ranges and needn't reach their ends.
Inputs may be any that keep to these rules, and one draw needn't show every extreme that they name: `gaps`: each row holds a start and an end with start <= end; some run is wholly a gap and some has none; gap density varies from region to region.
All inputs are finite; a program needn't handle non-finite values.
Results may differ from the reference program's by a relative error of at most 0.0058.
Values may be sent and summed in bfloat16 or wider, within the bound.
A program may use at most 64 MiB of HBM per device.

```python
import jax
import jax.numpy as jnp
from jax import lax

C = 512
PROJ = 1024
DILATION_BINS = 32
LAYERS = 2
BINS = 1024
HAPS = 4
BLOCKS = 8


def draw_gaps(key, part):
    key = jax.random.fold_in(key, 7)
    key_rate, key_take, key_length, key_start = jax.random.split(key, 4)
    region_rate = jax.random.randint(key_rate, (BLOCKS // 4,), 0, 4)
    block_rate = jnp.repeat(region_rate, 4)
    chosen = jax.random.randint(key_take, (BLOCKS,), 0, 4) < block_rate
    length = jnp.where(chosen, jax.random.randint(key_length, (BLOCKS,), 1, 129), 0)
    length = length.at[0].set(0).at[1].set(0).at[BLOCKS - 1].set(128)
    start = jax.random.randint(key_start, (BLOCKS,), 0, 129 - length)
    return jnp.stack([start, start + length], 1).astype(jnp.int32)


def spiked(values, rng, source, target, parts, factor):
    owner, partner = [(jnp.arange(values.shape[axis_at]) // (values.shape[axis_at] // parts)).reshape([-1 if axis == axis_at else 1 for axis in range(values.ndim)]) for axis_at in (source, target)]
    chosen = jax.random.permutation(rng, parts)[partner]
    strong = (owner == chosen) | (owner == (partner + parts // 2) % parts)
    return jnp.where(strong, factor * values, values)


def steps_of(own_key, shape, pieces, low, top_value):
    factor_of, own = 1.0, jax.random.fold_in(own_key, 6)
    for axis_at, shards_of in pieces:
        heights = jnp.exp(jax.random.uniform(jax.random.fold_in(own, axis_at), (shards_of,), jnp.float32, low / len(pieces), top_value / len(pieces)))
        factor_of = factor_of * jnp.repeat(heights, shape[axis_at] // shards_of).reshape([-1 if axis == axis_at else 1 for axis in range(len(shape))])
    return factor_of


def bell_draw(stream_key, extent, width, most, cuts=(), held_as=jnp.bfloat16):
    result = width * jax.random.normal(stream_key, extent, jnp.float32)
    if cuts:
        result = result * steps_of(stream_key, extent, cuts, -0.22, 0.18)
    return jnp.clip(result, -most, most).astype(held_as)


def noise_with(rng, dims, width, bound, shards, heavy, kind=jnp.bfloat16):
    drawn = width * jax.random.normal(rng, dims, jnp.float32)
    if shards:
        drawn = drawn * steps_of(rng, dims, shards, -0.22, 0.18)
    return jnp.clip(spiked(drawn, jax.random.fold_in(rng, 3), *heavy), -bound, bound).astype(kind)


def setup_inputs(seed: int = 0) -> dict:
    splits = jax.random.split(jax.random.key(seed), 7)
    tokens = noise_with(splits[0], (HAPS, BINS, C), 1.0, 6.0, ((0, 4), (1, 8)), (1, 2, 8, 2.0))
    cotangent = bell_draw(splits[1], (HAPS, BINS, C), 1.0, 6.0, ((0, 4), (1, 8)))
    gaps = draw_gaps(jax.random.fold_in(splits[6], 71), 0)
    conv_taps = bell_draw(splits[3], (LAYERS, 3, C), 3 ** -0.5, 3.5, (), jnp.float32)
    norm_gains = jnp.clip(1.0 + 0.15 * jax.random.normal(splits[4], (LAYERS, C), jnp.float32), 0.25, 1.75)
    projection = bell_draw(splits[5], (LAYERS, C, PROJ), C ** -0.5, 0.25)
    return {"tokens": tokens, "cotangent": cotangent, "gaps": gaps, "conv_taps": conv_taps, "norm_gains": norm_gains, "projection": projection}


EPS = 1e-06

def valid_of(gap_rows):
    offsets = jnp.arange(128, dtype=jnp.int32)[None, :]
    inside = (offsets >= gap_rows[:, 0:1]) & (offsets < gap_rows[:, 1:2])
    return jnp.where(inside, 0.0, 1.0).astype(jnp.float32).reshape(-1)

def forward_shift(values, offset):
    filler = jnp.zeros((abs(offset), values.shape[1]), values.dtype)
    if offset > 0:
        return jnp.concatenate([values[offset:], filler], 0)
    return jnp.concatenate([filler, values[:offset]], 0)

def norm_part(inputs, valid, gain):
    scaled = inputs.astype(jnp.float32)
    inv_rms = lax.rsqrt(lax.optimization_barrier(jnp.mean(scaled * scaled, axis=-1, keepdims=True)) + EPS)
    return (scaled, inv_rms, scaled * inv_rms * gain * valid[:, None])

def project(preactivation, weight):
    hidden = jax.nn.gelu(preactivation).astype(jnp.bfloat16)
    proj_out = jnp.dot(hidden, weight, preferred_element_type=jnp.float32)
    halfway = weight.shape[1] // 2
    return (hidden, proj_out[:, :halfway], jax.nn.sigmoid(proj_out[:, halfway:]))

def one_track(pair, valid, conv_taps, norm_gains, projection):
    current, grad_in = pair
    stored = []
    for layer in range(LAYERS):
        filter_weight = conv_taps[layer]
        scaled, inv_rms, normalized_tracks = norm_part(current, valid, norm_gains[layer])
        preactivation = filter_weight[0] * forward_shift(normalized_tracks, -DILATION_BINS) + filter_weight[1] * normalized_tracks + filter_weight[2] * forward_shift(normalized_tracks, DILATION_BINS)
        hidden, first, gate = project(preactivation, projection[layer])
        current = (scaled + valid[:, None] * first * gate).astype(jnp.bfloat16)
        stored.append((scaled, inv_rms, normalized_tracks, preactivation, hidden, first, gate))
    grad = grad_in.astype(jnp.float32)
    proj_terms, filter_tap_products, gain_terms = ([], [], [])
    for layer in reversed(range(LAYERS)):
        scaled, inv_rms, normalized_tracks, preactivation, hidden, first, gate = stored[layer]
        filter_weight = conv_taps[layer]
        branch = valid[:, None] * grad
        dproj = jnp.concatenate([branch * gate, branch * first * gate * (1.0 - gate)], 1).astype(jnp.bfloat16)
        dhidden = lax.dot_general(dproj, projection[layer], (((1,), (1,)), ((), ())), preferred_element_type=jnp.float32)
        proj_terms.append(lax.dot_general(hidden, dproj, (((0,), (0,)), ((), ())), preferred_element_type=jnp.float32))
        preactivation_gradient = jax.vjp(jax.nn.gelu, preactivation)[1](dhidden)[0]
        normalized_gradient = filter_weight[0] * forward_shift(preactivation_gradient, DILATION_BINS) + filter_weight[1] * preactivation_gradient + filter_weight[2] * forward_shift(preactivation_gradient, -DILATION_BINS)
        filter_tap_products.append(jnp.stack([lax.optimization_barrier(jnp.sum(preactivation_gradient * forward_shift(normalized_tracks, -DILATION_BINS), 0)), lax.optimization_barrier(jnp.sum(preactivation_gradient * normalized_tracks, 0)), lax.optimization_barrier(jnp.sum(preactivation_gradient * forward_shift(normalized_tracks, DILATION_BINS), 0))]))
        dq = normalized_gradient * valid[:, None]
        gain_terms.append(lax.optimization_barrier(jnp.sum(dq * scaled * inv_rms, 0)))
        dt = dq * norm_gains[layer]
        grad = grad + inv_rms * dt - scaled * inv_rms ** 3 * lax.optimization_barrier(jnp.mean(dt * scaled, axis=-1, keepdims=True))
    return (grad.astype(jnp.bfloat16), jnp.stack(proj_terms[::-1]), jnp.stack(filter_tap_products[::-1]), jnp.stack(gain_terms[::-1]))

def reference(tokens, cotangent, gaps, conv_taps, norm_gains, projection):
    valid = valid_of(gaps)
    results = lax.map(lambda pair: one_track(pair, valid, conv_taps, norm_gains, projection), (tokens, cotangent))
    tokens_grad, proj_terms, filter_tap_products, gain_terms = results
    return (tokens_grad, lax.optimization_barrier(jnp.sum(proj_terms, 0)), lax.optimization_barrier(jnp.sum(filter_tap_products, 0)), lax.optimization_barrier(jnp.sum(gain_terms, 0)))
```

```python
import functools

import jax
import jax.numpy as jnp
from jax import lax
from jax.experimental import pallas as pl
from jax.experimental.pallas import tpu as pltpu
from jax.sharding import PartitionSpec as P

D = 32
LAYERS = 2
EPS = 1e-06
GELU_C = 0.7978845608028654
GELU_A = 0.044715
F32 = jnp.float32
BF16 = jnp.bfloat16
MESH = pl.DeviceIdType.MESH


def kernel(
    n, haps, inside,
    tok, cot, gaps, taps, gains, w_hbm,
    tg_out, pg_out, sm_out,
    w, wsem, edge_out, halo_in, hs, hr, xs, inv, npad, dgelu, hid, proj, dp, dpad, gcur,
    hT, hTs, hTr, dq_in, dqs, dqr, gbf, rs, rss, rsr, ag, ags, agr, smh, smhs, smhr, sms, smss, smsr,
):
    me, h = lax.axis_index("seq"), lax.axis_index("hap")
    N, C = tok.shape
    PR = w.shape[2]
    Q = PR // haps
    chunks = N // D
    outer, inner = (0, chunks - 1), tuple(range(1, chunks - 1))
    rows = C // n
    left, right = jnp.maximum(me - 1, 0), jnp.minimum(me + 1, n - 1)
    has_left, has_right = me > 0, me < n - 1
    sends = []

    loads = [pltpu.make_async_copy(w_hbm.at[l], w.at[l], wsem.at[l]) for l in range(LAYERS)]
    for c in loads:
        c.start()

    barrier = pltpu.get_barrier_semaphore()
    if inside:
        for d in range(1, n):
            pl.semaphore_signal(barrier, inc=1, device_id={"seq": lax.rem(me + d, n)}, device_id_type=MESH)
        for d in range(1, haps):
            pl.semaphore_signal(barrier, inc=1, device_id={"hap": lax.rem(h + d, haps)}, device_id_type=MESH)
    else:
        @pl.when(has_left)
        def _():
            pl.semaphore_signal(barrier, inc=1, device_id={"seq": left}, device_id_type=MESH)

        @pl.when(has_right)
        def _():
            pl.semaphore_signal(barrier, inc=1, device_id={"seq": right}, device_id_type=MESH)

    offs = lax.broadcasted_iota(jnp.int32, (D, 1), 0)

    def valid_of(i):
        b = offs + i * D
        return jnp.where((b >= gaps[0, 0]) & (b < gaps[0, 1]), 0.0, 1.0).astype(F32)

    valid = [valid_of(i) for i in range(chunks)]

    def ds(i):
        return pl.ds(i * D, D)

    def halo(k):
        up = pltpu.make_async_remote_copy(
            src_ref=edge_out.at[k, 1], dst_ref=halo_in.at[k, 0], send_sem=hs.at[k, 1],
            recv_sem=hr.at[k, 0], device_id={"seq": right}, device_id_type=MESH)
        down = pltpu.make_async_remote_copy(
            src_ref=edge_out.at[k, 0], dst_ref=halo_in.at[k, 1], send_sem=hs.at[k, 0],
            recv_sem=hr.at[k, 1], device_id={"seq": left}, device_id_type=MESH)
        return up, down

    def halo_start(k):
        up, down = halo(k)

        @pl.when(has_right)
        def _():
            up.start()

        @pl.when(has_left)
        def _():
            down.start()

        @pl.when(jnp.logical_not(has_left))
        def _():
            halo_in[k, 0] = jnp.zeros((D, C), BF16)

        @pl.when(jnp.logical_not(has_right))
        def _():
            halo_in[k, 1] = jnp.zeros((D, C), BF16)

    def halo_wait(k):
        up, down = halo(k)

        @pl.when(has_left)
        def _():
            up.wait_recv()

        @pl.when(has_right)
        def _():
            down.wait_recv()

    def halo_drain(k):
        up, down = halo(k)

        @pl.when(has_right)
        def _():
            up.wait_send()

        @pl.when(has_left)
        def _():
            down.wait_send()

    def to_hap(src_of, dst_of, ss, rr):
        out = []
        for d in range(1, haps):
            t = lax.rem(h + d, haps)
            c = pltpu.make_async_remote_copy(
                src_ref=src_of(t), dst_ref=dst_of(d), send_sem=ss(d), recv_sem=rr(d),
                device_id={"hap": t}, device_id_type=MESH)
            c.start()
            out.append(c)
        sends.extend(out)
        return out

    def to_seq(src_of, dst_of, ss, rr):
        out = []
        for d in range(1, n):
            t = lax.rem(me + d, n)
            c = pltpu.make_async_remote_copy(
                src_ref=src_of(t), dst_ref=dst_of(d), send_sem=ss(d), recv_sem=rr(d),
                device_id={"seq": t}, device_id_type=MESH)
            c.start()
            out.append(c)
        sends.extend(out)
        return out

    xs[0] = tok[...]
    edge_out[0, 0] = (tok[ds(0), :].astype(F32) * valid[0]).astype(BF16)
    edge_out[0, 1] = (tok[ds(chunks - 1), :].astype(F32) * valid[-1]).astype(BF16)
    if inside:
        pl.semaphore_wait(barrier, n - 1 + haps - 1)
    else:
        @pl.when(has_left)
        def _():
            pl.semaphore_wait(barrier, 1)

        @pl.when(has_right)
        def _():
            pl.semaphore_wait(barrier, 1)
    halo_start(0)

    def rms(x):
        return lax.rsqrt(jnp.mean(x * x, axis=-1, keepdims=True) + EPS)

    def forward_chunk(l, i):
        pre = (
            taps[l, 0:1, :] * npad[l, ds(i), :]
            + taps[l, 1:2, :] * npad[l, ds(i + 1), :]
            + taps[l, 2:3, :] * npad[l, ds(i + 2), :]
        )
        sq = pre * pre
        th = jnp.tanh(GELU_C * (pre + GELU_A * (sq * pre)))
        half = 0.5 * (1.0 + th)
        hidden = (pre * half).astype(BF16)
        hid[l, ds(i), :] = hidden
        dgelu[l, ds(i), :] = half + 0.5 * pre * (1.0 - th * th) * (GELU_C * (1.0 + 3.0 * GELU_A * sq))

    hT_copies = [None] * LAYERS
    for l in range(LAYERS):
        gain = gains[l : l + 1, :]
        for i in range(chunks):
            x = xs[l, ds(i), :].astype(F32)
            r = rms(x)
            inv[l, ds(i), :] = r
            npad[l, ds(i + 1), :] = x * r * gain * valid[i]
        for i in inner:
            forward_chunk(l, i)
        halo_wait(l)
        for side, at in ((0, 0), (1, chunks + 1)):
            x = halo_in[l, side].astype(F32)
            npad[l, ds(at), :] = x * rms(x) * gain
        for i in outer:
            forward_chunk(l, i)
        loads[l].wait()
        proj[l] = jnp.dot(hid[l], w[l], preferred_element_type=F32)
        if l + 1 < LAYERS:
            for i in outer + inner:
                first = proj[l, ds(i), 0:C]
                gate = jax.nn.sigmoid(proj[l, ds(i), C:PR])
                proj[l, ds(i), C:PR] = gate
                nxt = (xs[l, ds(i), :].astype(F32) + valid[i] * first * gate).astype(BF16)
                xs[l + 1, ds(i), :] = nxt
                if i in outer:
                    edge_out[l + 1, 0 if i == 0 else 1] = (nxt.astype(F32) * valid[i]).astype(BF16)
                if i == outer[-1]:
                    halo_start(l + 1)
        hT[l, :, 0:N] = jnp.transpose(hid[l].astype(F32)).astype(BF16)
        if inside:
            hT_copies[l] = to_hap(
                lambda t: hT.at[l, :, pl.ds(0, N)], lambda d: hT.at[l, :, pl.ds(d * N, N)],
                lambda d: hTs.at[l, d], lambda d: hTr.at[l, d])

    dq_copies, rs_copies, ag_copies = [None] * LAYERS, [None] * LAYERS, [None] * LAYERS

    def gram(l):
        if not inside:
            pg_out[l] = jnp.dot(hT[l], dp[l], preferred_element_type=F32)
            return
        dq_in[l, 0:N, :] = dp[l, :, pl.ds(pl.multiple_of(h * Q, Q), Q)]
        for c in hT_copies[l] + dq_copies[l]:
            c.wait_recv()
        g = jnp.dot(hT[l], dq_in[l], preferred_element_type=F32)
        gbf[l] = g.astype(BF16).reshape(n, rows, Q)
        rs_copies[l] = to_seq(
            lambda t: gbf.at[l, t], lambda d: rs.at[l, d], lambda d: rss.at[l, d], lambda d: rsr.at[l, d])

    def reduced(l):
        total = gbf[l, me].astype(F32)
        for c in rs_copies[l]:
            c.wait_recv()
        for d in range(1, n):
            total = total + rs[l, d].astype(F32)
        ag[l, h] = total.astype(BF16)
        ag_copies[l] = to_hap(
            lambda t: ag.at[l, h], lambda d: ag.at[l, h], lambda d: ags.at[l, d], lambda d: agr.at[l, d])

    for l in reversed(range(LAYERS)):
        k = 2 * LAYERS - 1 - l
        last = l == LAYERS - 1
        gain = gains[l : l + 1, :]
        for i in range(chunks):
            first = proj[l, ds(i), 0:C]
            gate = proj[l, ds(i), C:PR]
            if last:
                gate = jax.nn.sigmoid(gate)
            grad = cot[ds(i), :].astype(F32) if last else gcur[ds(i), :]
            branch = valid[i] * grad
            bg = branch * gate
            dp[l, ds(i), 0:C] = bg.astype(BF16)
            dp[l, ds(i), C:PR] = (bg * first * (1.0 - gate)).astype(BF16)
        if inside:
            dq_copies[l] = to_hap(
                lambda t: dp.at[l, :, pl.ds(pl.multiple_of(t * Q, Q), Q)],
                lambda d: dq_in.at[l, pl.ds(d * N, N), :],
                lambda d: dqs.at[l, d], lambda d: dqr.at[l, d])
        dpad[l, pl.ds(D, N), :] = lax.dot_general(
            dp[l], w[l], (((1,), (1,)), ((), ())), preferred_element_type=F32)
        t_sum = [jnp.zeros((1, C), F32) for _ in range(3)]
        for i in outer + inner:
            dpre = dpad[l, ds(i + 1), :] * dgelu[l, ds(i), :]
            dpad[l, ds(i + 1), :] = dpre
            if i in outer:
                edge_out[k, 0 if i == 0 else 1] = dpre.astype(BF16)
            if i == outer[-1]:
                halo_start(k)
            for j in range(3):
                t_sum[j] = t_sum[j] + jnp.sum(dpre * npad[l, ds(i + j), :], axis=0, keepdims=True)
        g_sum = jnp.zeros((1, C), F32)

        def back_chunk(i, g_sum):
            dn = (
                taps[l, 0:1, :] * dpad[l, ds(i + 2), :]
                + taps[l, 1:2, :] * dpad[l, ds(i + 1), :]
                + taps[l, 2:3, :] * dpad[l, ds(i), :]
            )
            dq = dn * valid[i]
            x = xs[l, ds(i), :].astype(F32)
            r = inv[l, ds(i), :]
            xr = x * r
            g_sum = g_sum + jnp.sum(dq * xr, axis=0, keepdims=True)
            dt = dq * gain
            grad = cot[ds(i), :].astype(F32) if last else gcur[ds(i), :]
            new = grad + r * dt - xr * (r * r * jnp.mean(dt * x, axis=-1, keepdims=True))
            if l == 0:
                tg_out[ds(i), :] = new
            else:
                gcur[ds(i), :] = new
            return g_sum

        for i in inner:
            g_sum = back_chunk(i, g_sum)
        gram(l)
        halo_wait(k)
        dpad[l, ds(0), :] = halo_in[k, 0].astype(F32)
        dpad[l, ds(chunks + 1), :] = halo_in[k, 1].astype(F32)
        for i in outer:
            g_sum = back_chunk(i, g_sum)
        for j in range(3):
            smh[h, 3 * l + j : 3 * l + j + 1, :] = t_sum[j]
        smh[h, 3 * LAYERS + l : 3 * LAYERS + l + 1, :] = g_sum

    if inside:
        small = to_hap(lambda t: smh.at[h], lambda d: smh.at[h], lambda d: smhs.at[d], lambda d: smhr.at[d])
        reduced(LAYERS - 1)
        for c in small:
            c.wait_recv()
        total = smh[0]
        for q in range(1, haps):
            total = total + smh[q]
        sms[me] = total
        small = to_seq(lambda t: sms.at[me], lambda d: sms.at[me], lambda d: smss.at[d], lambda d: smsr.at[d])
        for l in reversed(range(LAYERS - 1)):
            reduced(l)
        for c in small:
            c.wait_recv()
        total = sms[0]
        for s in range(1, n):
            total = total + sms[s]
        sm_out[...] = total
        for l in reversed(range(LAYERS)):
            for c in ag_copies[l]:
                c.wait_recv()
            for q in range(haps):
                pg_out[l, :, q * Q : (q + 1) * Q] = ag[l, q]
    else:
        sm_out[...] = smh[h]
    for k in range(2 * LAYERS):
        halo_drain(k)
    for c in sends:
        c.wait_send()


def shards(n, haps, tokens, cotangent, gaps, conv_taps, norm_gains, projection):
    x = tokens[0]
    N, C = x.shape
    PR = projection.shape[2]
    inside = n > 1 and haps > 1 and C % (16 * n) == 0 and PR % (128 * haps) == 0
    Q, rows = PR // haps, max(C // n, 1)
    L = LAYERS
    wide = haps if inside else 1

    def dma(*shape):
        return pltpu.SemaphoreType.DMA(shape)

    def opt(shape, dtype):
        return pltpu.VMEM(shape if inside else (16, 128), dtype)

    scratch = [
        pltpu.VMEM((L, C, PR), BF16), dma(L),
        pltpu.VMEM((2 * L, 2, D, C), BF16), pltpu.VMEM((2 * L, 2, D, C), BF16), dma(2 * L, 2), dma(2 * L, 2),
        pltpu.VMEM((L, N, C), BF16), pltpu.VMEM((L, N, 1), F32), pltpu.VMEM((L, N + 2 * D, C), F32),
        pltpu.VMEM((L, N, C), F32), pltpu.VMEM((L, N, C), BF16), pltpu.VMEM((L, N, PR), F32),
        pltpu.VMEM((L, N, PR), BF16), pltpu.VMEM((L, N + 2 * D, C), F32), pltpu.VMEM((N, C), F32),
        pltpu.VMEM((L, C, N * wide), BF16), dma(L, haps), dma(L, haps),
        opt((L, N * haps, Q), BF16), dma(L, haps), dma(L, haps),
        opt((L, n, rows, Q), BF16), opt((L, n, rows, Q), BF16), dma(L, n), dma(L, n),
        opt((L, haps, rows, Q), BF16), dma(L, haps), dma(L, haps),
        pltpu.VMEM((haps, 4 * L, C), F32), dma(haps), dma(haps),
        opt((n, 4 * L, C), F32), dma(n), dma(n),
    ]
    vmem = pl.BlockSpec(memory_space=pltpu.VMEM)
    pg_shape = jax.ShapeDtypeStruct((L, rows, PR), BF16) if inside else jax.ShapeDtypeStruct((L, C, PR), F32)
    tg, pg, sm = pl.pallas_call(
        functools.partial(kernel, n, haps, inside),
        out_shape=[jax.ShapeDtypeStruct((N, C), F32), pg_shape, jax.ShapeDtypeStruct((4 * L, C), F32)],
        in_specs=[vmem, vmem, pl.BlockSpec(memory_space=pltpu.SMEM), vmem, vmem, pl.BlockSpec(memory_space=pl.ANY)],
        out_specs=[vmem] * 3,
        scratch_shapes=scratch,
        compiler_params=pltpu.CompilerParams(
            collective_id=0, has_side_effects=True, vmem_limit_bytes=48 * 1024 * 1024),
    )(x, cotangent[0], gaps, conv_taps, norm_gains, projection)
    if inside:
        pg = pg.astype(F32)
    else:
        pg = lax.psum(lax.psum_scatter(pg, "seq", scatter_dimension=1, tiled=True), "hap")
        sm = lax.psum(sm, ("seq", "hap"))
    return tg.astype(BF16)[None], pg, sm[: 3 * L].reshape(L, 3, C), sm[3 * L :]


def solution(mesh):
    return jax.shard_map(
        functools.partial(shards, mesh.shape["seq"], mesh.shape["hap"]),
        mesh=mesh,
        in_specs=(P("hap", "seq", None), P("hap", "seq", None), P("seq", None), P(), P(), P()),
        out_specs=(P("hap", "seq", None), P(None, "seq", None), P(), P()),
        check_vma=False,
    )
```

```python
import functools

import jax
import jax.numpy as jnp
from jax import lax
from jax.experimental import pallas as pl
from jax.experimental.pallas import tpu as pltpu
from jax.sharding import PartitionSpec as P

D = 32
LAYERS = 2
EPS = 1e-06
GELU_C = 0.7978845608028654
GELU_A = 0.044715
F32 = jnp.float32
BF16 = jnp.bfloat16
MESH = pl.DeviceIdType.MESH


def kernel(
    n, haps, inside,
    tok_hbm, cot_hbm, gaps_hbm, taps_hbm, gains_hbm, w_hbm,
    tg_out, pg_out, sm_out,
    tok, cot, gaps, taps, gains, isem, w, wsem, edge_out, halo_in, hs, hr, xs, inv, npad, dgelu, hid, proj, dp, dpad, gcur,
    hT, hTs, hTr, dq_in, dqs, dqr, gbf, rs, rss, rsr, ag, ags, agr, smh, smhs, smhr, sms, smss, smsr,
):
    me, h = lax.axis_index("seq"), lax.axis_index("hap")
    N, C = tok.shape
    PR = w.shape[2]
    Q = PR // haps
    chunks = N // D
    outer, inner = (0, chunks - 1), tuple(range(1, chunks - 1))
    rows = C // n
    left, right = jnp.maximum(me - 1, 0), jnp.minimum(me + 1, n - 1)
    has_left, has_right = me > 0, me < n - 1
    sends = []

    loads = [pltpu.make_async_copy(w_hbm.at[l], w.at[l], wsem.at[l]) for l in range(LAYERS)]
    small_in = [
        pltpu.make_async_copy(a, b, isem.at[j])
        for j, (a, b) in enumerate(
            ((tok_hbm, tok), (gaps_hbm, gaps), (gains_hbm, gains), (taps_hbm, taps), (cot_hbm, cot)))
    ]
    for c in small_in[:4] + loads + small_in[4:]:
        c.start()

    barrier = pltpu.get_barrier_semaphore()
    if inside:
        for d in range(1, n):
            pl.semaphore_signal(barrier, inc=1, device_id={"seq": lax.rem(me + d, n)}, device_id_type=MESH)
        for d in range(1, haps):
            pl.semaphore_signal(barrier, inc=1, device_id={"hap": lax.rem(h + d, haps)}, device_id_type=MESH)
    else:
        @pl.when(has_left)
        def _():
            pl.semaphore_signal(barrier, inc=1, device_id={"seq": left}, device_id_type=MESH)

        @pl.when(has_right)
        def _():
            pl.semaphore_signal(barrier, inc=1, device_id={"seq": right}, device_id_type=MESH)

    offs = lax.broadcasted_iota(jnp.int32, (D, 1), 0)

    def valid_of(i):
        b = offs + i * D
        return jnp.where((b >= gaps[0, 0]) & (b < gaps[0, 1]), 0.0, 1.0).astype(F32)

    small_in[0].wait()
    small_in[1].wait()
    valid = [valid_of(i) for i in range(chunks)]

    def ds(i):
        return pl.ds(i * D, D)

    def halo(k):
        up = pltpu.make_async_remote_copy(
            src_ref=edge_out.at[k, 1], dst_ref=halo_in.at[k, 0], send_sem=hs.at[k, 1],
            recv_sem=hr.at[k, 0], device_id={"seq": right}, device_id_type=MESH)
        down = pltpu.make_async_remote_copy(
            src_ref=edge_out.at[k, 0], dst_ref=halo_in.at[k, 1], send_sem=hs.at[k, 0],
            recv_sem=hr.at[k, 1], device_id={"seq": left}, device_id_type=MESH)
        return up, down

    def halo_start(k):
        up, down = halo(k)

        @pl.when(has_right)
        def _():
            up.start()

        @pl.when(has_left)
        def _():
            down.start()

        @pl.when(jnp.logical_not(has_left))
        def _():
            halo_in[k, 0] = jnp.zeros((D, C), BF16)

        @pl.when(jnp.logical_not(has_right))
        def _():
            halo_in[k, 1] = jnp.zeros((D, C), BF16)

    def halo_wait(k):
        up, down = halo(k)

        @pl.when(has_left)
        def _():
            up.wait_recv()

        @pl.when(has_right)
        def _():
            down.wait_recv()

    def halo_drain(k):
        up, down = halo(k)

        @pl.when(has_right)
        def _():
            up.wait_send()

        @pl.when(has_left)
        def _():
            down.wait_send()

    def to_hap(src_of, dst_of, ss, rr):
        out = []
        for d in range(1, haps):
            t = lax.rem(h + d, haps)
            c = pltpu.make_async_remote_copy(
                src_ref=src_of(t), dst_ref=dst_of(d), send_sem=ss(d), recv_sem=rr(d),
                device_id={"hap": t}, device_id_type=MESH)
            c.start()
            out.append(c)
        sends.extend(out)
        return out

    def to_seq(src_of, dst_of, ss, rr):
        out = []
        for d in range(1, n):
            t = lax.rem(me + d, n)
            c = pltpu.make_async_remote_copy(
                src_ref=src_of(t), dst_ref=dst_of(d), send_sem=ss(d), recv_sem=rr(d),
                device_id={"seq": t}, device_id_type=MESH)
            c.start()
            out.append(c)
        sends.extend(out)
        return out

    xs[0] = tok[...]
    edge_out[0, 0] = (tok[ds(0), :].astype(F32) * valid[0]).astype(BF16)
    edge_out[0, 1] = (tok[ds(chunks - 1), :].astype(F32) * valid[-1]).astype(BF16)
    if inside:
        pl.semaphore_wait(barrier, n - 1 + haps - 1)
    else:
        @pl.when(has_left)
        def _():
            pl.semaphore_wait(barrier, 1)

        @pl.when(has_right)
        def _():
            pl.semaphore_wait(barrier, 1)
    halo_start(0)
    small_in[2].wait()
    small_in[3].wait()

    def rms(x):
        return lax.rsqrt(jnp.mean(x * x, axis=-1, keepdims=True) + EPS)

    def forward_chunk(l, i):
        pre = (
            taps[0, l : l + 1, :] * npad[l, ds(i), :]
            + taps[1, l : l + 1, :] * npad[l, ds(i + 1), :]
            + taps[2, l : l + 1, :] * npad[l, ds(i + 2), :]
        )
        sq = pre * pre
        th = jnp.tanh(GELU_C * (pre + GELU_A * (sq * pre)))
        half = 0.5 * (1.0 + th)
        hidden = (pre * half).astype(BF16)
        hid[l, ds(i), :] = hidden
        dgelu[l, ds(i), :] = half + 0.5 * pre * (1.0 - th * th) * (GELU_C * (1.0 + 3.0 * GELU_A * sq))

    hT_copies = [None] * LAYERS

    def send_hidden(l):
        hT[l, :, 0:N] = jnp.transpose(hid[l].astype(F32)).astype(BF16)
        if inside:
            hT_copies[l] = to_hap(
                lambda t: hT.at[l, :, pl.ds(0, N)], lambda d: hT.at[l, :, pl.ds(d * N, N)],
                lambda d: hTs.at[l, d], lambda d: hTr.at[l, d])

    for l in range(LAYERS):
        gain = gains[l : l + 1, :]
        for i in range(chunks):
            x = xs[l, ds(i), :].astype(F32)
            r = rms(x)
            inv[l, ds(i), :] = r
            npad[l, ds(i + 1), :] = x * r * gain * valid[i]
        for i in inner:
            forward_chunk(l, i)
        halo_wait(l)
        for side, at in ((0, 0), (1, chunks + 1)):
            x = halo_in[l, side].astype(F32)
            npad[l, ds(at), :] = x * rms(x) * gain
        for i in outer:
            forward_chunk(l, i)
        loads[l].wait()
        proj[l] = jnp.dot(hid[l], w[l], preferred_element_type=F32)
        if l + 1 < LAYERS:
            for i in outer + inner:
                first = proj[l, ds(i), 0:C]
                gate = jax.nn.sigmoid(proj[l, ds(i), C:PR])
                proj[l, ds(i), C:PR] = gate
                nxt = (xs[l, ds(i), :].astype(F32) + valid[i] * first * gate).astype(BF16)
                xs[l + 1, ds(i), :] = nxt
                if i in outer:
                    edge_out[l + 1, 0 if i == 0 else 1] = (nxt.astype(F32) * valid[i]).astype(BF16)
                if i == outer[-1]:
                    halo_start(l + 1)
        if l + 1 < LAYERS:
            send_hidden(l)

    dq_copies, rs_copies, ag_copies = [[] for _ in range(LAYERS)], [None] * LAYERS, [None] * LAYERS

    def gram(l):
        if not inside:
            pg_out[l] = jnp.dot(hT[l], dp[l], preferred_element_type=F32)
            return
        dq_in[l, 0:N, :] = dp[l, :, pl.ds(pl.multiple_of(h * Q, Q), Q)]
        for c in hT_copies[l] + dq_copies[l]:
            c.wait_recv()
        g = jnp.dot(hT[l], dq_in[l], preferred_element_type=F32)
        gbf[l] = g.astype(BF16).reshape(n, rows, Q)
        rs_copies[l] = to_seq(
            lambda t: gbf.at[l, t], lambda d: rs.at[l, d], lambda d: rss.at[l, d], lambda d: rsr.at[l, d])

    def reduced(l):
        total = gbf[l, me].astype(F32)
        for c in rs_copies[l]:
            c.wait_recv()
        for d in range(1, n):
            total = total + rs[l, d].astype(F32)
        ag[l, h] = total.astype(BF16)
        ag_copies[l] = to_hap(
            lambda t: ag.at[l, h], lambda d: ag.at[l, h], lambda d: ags.at[l, d], lambda d: agr.at[l, d])

    def dproj(l, i):
        last = l == LAYERS - 1
        first = proj[l, ds(i), 0:C]
        gate = proj[l, ds(i), C:PR]
        if last:
            gate = jax.nn.sigmoid(gate)
        grad = cot[ds(i), :].astype(F32) if last else gcur[ds(i), :]
        bg = valid[i] * grad * gate
        dp[l, ds(i), 0:C] = bg.astype(BF16)
        dp[l, ds(i), C:PR] = (bg * first * (1.0 - gate)).astype(BF16)

    def send_dproj(l, j, start, size):
        if inside:
            dq_copies[l] += to_hap(
                lambda t: dp.at[l, pl.ds(start, size), pl.ds(pl.multiple_of(t * Q, Q), Q)],
                lambda d: dq_in.at[l, pl.ds(d * N + start, size), :],
                lambda d: dqs.at[l, d, j], lambda d: dqr.at[l, d, j])

    def fold(x):
        return jnp.sum(x.reshape(D // 8, 8, C), axis=0)

    small_in[4].wait()
    for i in range(chunks):
        dproj(LAYERS - 1, i)
    send_dproj(LAYERS - 1, 0, 0, N)
    for l in reversed(range(LAYERS)):
        k = 2 * LAYERS - 1 - l
        last = l == LAYERS - 1
        gain = gains[l : l + 1, :]
        if not last:
            gram(l + 1)
        dpad[l, pl.ds(D, N), :] = lax.dot_general(
            dp[l], w[l], (((1,), (1,)), ((), ())), preferred_element_type=F32)
        for i in outer + inner:
            dpre = dpad[l, ds(i + 1), :] * dgelu[l, ds(i), :]
            dpad[l, ds(i + 1), :] = dpre
            if i in outer:
                edge_out[k, 0 if i == 0 else 1] = dpre.astype(BF16)
            if i == outer[-1]:
                halo_start(k)
        if last:
            send_hidden(l)
        g_sum = jnp.zeros((8, C), F32)

        def back_chunk(i, g_sum):
            dn = (
                taps[0, l : l + 1, :] * dpad[l, ds(i + 2), :]
                + taps[1, l : l + 1, :] * dpad[l, ds(i + 1), :]
                + taps[2, l : l + 1, :] * dpad[l, ds(i), :]
            )
            dq = dn * valid[i]
            x = xs[l, ds(i), :].astype(F32)
            r = inv[l, ds(i), :]
            xr = x * r
            g_sum = g_sum + fold(dq * xr)
            dt = dq * gain
            grad = cot[ds(i), :].astype(F32) if last else gcur[ds(i), :]
            new = grad + r * dt - xr * (r * r * jnp.mean(dt * x, axis=-1, keepdims=True))
            if l == 0:
                tg_out[ds(i), :] = new.astype(BF16)
            else:
                gcur[ds(i), :] = new
                dproj(l - 1, i)
            return g_sum

        for i in inner:
            g_sum = back_chunk(i, g_sum)
        if l > 0:
            send_dproj(l - 1, 0, D, N - 2 * D)
        t_sum = [jnp.zeros((8, C), F32) for _ in range(3)]
        for i in range(chunks):
            dpre = dpad[l, ds(i + 1), :]
            for j in range(3):
                t_sum[j] = t_sum[j] + fold(dpre * npad[l, ds(i + j), :])
        for j in range(3):
            smh[h, LAYERS * j + l : LAYERS * j + l + 1, :] = jnp.sum(t_sum[j], axis=0, keepdims=True)
        if l == 0:
            gram(0)
        halo_wait(k)
        dpad[l, ds(0), :] = halo_in[k, 0].astype(F32)
        dpad[l, ds(chunks + 1), :] = halo_in[k, 1].astype(F32)
        for i in outer:
            g_sum = back_chunk(i, g_sum)
        if l > 0:
            send_dproj(l - 1, 1, 0, D)
            send_dproj(l - 1, 2, N - D, D)
        smh[h, 3 * LAYERS + l : 3 * LAYERS + l + 1, :] = jnp.sum(g_sum, axis=0, keepdims=True)

    if inside:
        small = to_hap(lambda t: smh.at[h], lambda d: smh.at[h], lambda d: smhs.at[d], lambda d: smhr.at[d])
        reduced(LAYERS - 1)
        for c in small:
            c.wait_recv()
        total = smh[0]
        for q in range(1, haps):
            total = total + smh[q]
        sms[me] = total
        small = to_seq(lambda t: sms.at[me], lambda d: sms.at[me], lambda d: smss.at[d], lambda d: smsr.at[d])
        for l in reversed(range(LAYERS - 1)):
            reduced(l)
        for c in small:
            c.wait_recv()
        total = sms[0]
        for s in range(1, n):
            total = total + sms[s]
        sm_out[...] = total
        for l in reversed(range(LAYERS)):
            for c in ag_copies[l]:
                c.wait_recv()
            for q in range(haps):
                pg_out[l, :, q * Q : (q + 1) * Q] = ag[l, q]
    else:
        sm_out[...] = smh[h]
    for k in range(2 * LAYERS):
        halo_drain(k)
    for c in sends:
        c.wait_send()


def finish(tg, pg, sm, tg_out, pg_out, taps_out, gains_out):
    L, C = gains_out.shape
    tg_out[...] = tg[...]
    pg_out[...] = pg[...].astype(F32)
    for j in range(3):
        taps_out[j] = sm[j * L : (j + 1) * L, :]
    gains_out[...] = sm[3 * L :, :]


def shards(n, haps, tokens, cotangent, gaps, conv_taps, norm_gains, projection):
    x = tokens[0]
    N, C = x.shape
    PR = projection.shape[2]
    inside = n > 1 and haps > 1 and C % (16 * n) == 0 and PR % (128 * haps) == 0
    Q, rows = PR // haps, max(C // n, 1)
    L = LAYERS
    wide = haps if inside else 1

    def dma(*shape):
        return pltpu.SemaphoreType.DMA(shape)

    def opt(shape, dtype):
        return pltpu.VMEM(shape if inside else (16, 128), dtype)

    scratch = [
        pltpu.VMEM((N, C), BF16), pltpu.VMEM((N, C), BF16), pltpu.SMEM(gaps.shape, jnp.int32),
        pltpu.VMEM((3, L, C), F32), pltpu.VMEM((L, C), F32), dma(5),
        pltpu.VMEM((L, C, PR), BF16), dma(L),
        pltpu.VMEM((2 * L, 2, D, C), BF16), pltpu.VMEM((2 * L, 2, D, C), BF16), dma(2 * L, 2), dma(2 * L, 2),
        pltpu.VMEM((L, N, C), BF16), pltpu.VMEM((L, N, 1), F32), pltpu.VMEM((L, N + 2 * D, C), F32),
        pltpu.VMEM((L, N, C), F32), pltpu.VMEM((L, N, C), BF16), pltpu.VMEM((L, N, PR), F32),
        pltpu.VMEM((L, N, PR), BF16), pltpu.VMEM((L, N + 2 * D, C), F32), pltpu.VMEM((N, C), F32),
        pltpu.VMEM((L, C, N * wide), BF16), dma(L, haps), dma(L, haps),
        opt((L, N * haps, Q), BF16), dma(L, haps, 3), dma(L, haps, 3),
        opt((L, n, rows, Q), BF16), opt((L, n, rows, Q), BF16), dma(L, n), dma(L, n),
        opt((L, haps, rows, Q), BF16), dma(L, haps), dma(L, haps),
        pltpu.VMEM((haps, 4 * L, C), F32), dma(haps), dma(haps),
        opt((n, 4 * L, C), F32), dma(n), dma(n),
    ]
    vmem = pl.BlockSpec(memory_space=pltpu.VMEM)
    hbm = pl.BlockSpec(memory_space=pltpu.HBM)
    pg_shape = jax.ShapeDtypeStruct((L, rows, PR), BF16) if inside else jax.ShapeDtypeStruct((L, C, PR), F32)
    tg, pg, sm = pl.pallas_call(
        functools.partial(kernel, n, haps, inside),
        out_shape=[jax.ShapeDtypeStruct((N, C), BF16), pg_shape, jax.ShapeDtypeStruct((4 * L, C), F32)],
        in_specs=[hbm] * 6,
        out_specs=[vmem] * 3,
        scratch_shapes=scratch,
        compiler_params=pltpu.CompilerParams(
            collective_id=0, has_side_effects=True, vmem_limit_bytes=60 * 1024 * 1024),
    )(x, cotangent[0], gaps, jnp.transpose(conv_taps, (1, 0, 2)), norm_gains, projection)
    if not inside:
        pg = lax.psum(lax.psum_scatter(pg, "seq", scatter_dimension=1, tiled=True), "hap")
        sm = lax.psum(sm, ("seq", "hap"))
    tg, pg, taps, gains = pl.pallas_call(
        finish,
        out_shape=[
            jax.ShapeDtypeStruct(tg.shape, BF16), jax.ShapeDtypeStruct(pg.shape, F32),
            jax.ShapeDtypeStruct((3, L, C), F32), jax.ShapeDtypeStruct((L, C), F32)],
        in_specs=[vmem] * 3,
        out_specs=[vmem] * 4,
        compiler_params=pltpu.CompilerParams(vmem_limit_bytes=8 * 1024 * 1024),
    )(tg, pg, sm)
    return tg[None], pg, jnp.transpose(taps, (1, 0, 2)), gains


def solution(mesh):
    return jax.shard_map(
        functools.partial(shards, mesh.shape["seq"], mesh.shape["hap"]),
        mesh=mesh,
        in_specs=(P("hap", "seq", None), P("hap", "seq", None), P("seq", None), P(), P(), P()),
        out_specs=(P("hap", "seq", None), P(None, "seq", None), P(), P()),
        check_vma=False,
    )
```

```python
import functools

import jax
import jax.numpy as jnp
from jax import lax
from jax.experimental import pallas as pl
from jax.experimental.pallas import tpu as pltpu
from jax.sharding import PartitionSpec as P

D = 32
LAYERS = 2
EPS = 1e-06
GELU_C = 0.7978845608028654
GELU_A = 0.044715
F32 = jnp.float32
BF16 = jnp.bfloat16
MESH = pl.DeviceIdType.MESH


def kernel(
    n, haps, inside,
    tok_hbm, cot_hbm, gaps_hbm, taps_hbm, gains_hbm, w_hbm,
    tg_hbm, pg_hbm, tp_hbm, gn_hbm,
    tg_out, pg_out, tp_out, gn_out, osem, tok, cot, gaps, taps, gains, isem, w, wsem, edge_out, halo_in, hs, hr, xs, inv, npad, dgelu, hid, proj, dp, dpad, gcur,
    hT, hTs, hTr, dq_in, dqs, dqr, gbf, rs, rss, rsr, ag, ags, agr, smh, smhs, smhr, sms, smss, smsr,
):
    me, h = lax.axis_index("seq"), lax.axis_index("hap")
    N, C = tok.shape
    PR = w.shape[2]
    Q = PR // haps
    chunks = N // D
    outer, inner = (0, chunks - 1), tuple(range(1, chunks - 1))
    rows = C // n
    left, right = jnp.maximum(me - 1, 0), jnp.minimum(me + 1, n - 1)
    has_left, has_right = me > 0, me < n - 1
    sends = []

    loads = [pltpu.make_async_copy(w_hbm.at[l], w.at[l], wsem.at[l]) for l in range(LAYERS)]
    small_in = [
        pltpu.make_async_copy(a, b, isem.at[j])
        for j, (a, b) in enumerate(
            ((tok_hbm, tok), (gaps_hbm, gaps), (gains_hbm, gains), (taps_hbm, taps), (cot_hbm, cot)))
    ]
    for c in small_in[:4] + loads + small_in[4:]:
        c.start()

    barrier = pltpu.get_barrier_semaphore()
    if inside:
        for d in range(1, n):
            pl.semaphore_signal(barrier, inc=1, device_id={"seq": lax.rem(me + d, n)}, device_id_type=MESH)
        for d in range(1, haps):
            pl.semaphore_signal(barrier, inc=1, device_id={"hap": lax.rem(h + d, haps)}, device_id_type=MESH)
    else:
        @pl.when(has_left)
        def _():
            pl.semaphore_signal(barrier, inc=1, device_id={"seq": left}, device_id_type=MESH)

        @pl.when(has_right)
        def _():
            pl.semaphore_signal(barrier, inc=1, device_id={"seq": right}, device_id_type=MESH)

    offs = lax.broadcasted_iota(jnp.int32, (D, 1), 0)

    def valid_of(i):
        b = offs + i * D
        return jnp.where((b >= gaps[0, 0]) & (b < gaps[0, 1]), 0.0, 1.0).astype(F32)

    small_in[0].wait()
    small_in[1].wait()
    valid = [valid_of(i) for i in range(chunks)]

    def ds(i):
        return pl.ds(i * D, D)

    def halo(k):
        up = pltpu.make_async_remote_copy(
            src_ref=edge_out.at[k, 1], dst_ref=halo_in.at[k, 0], send_sem=hs.at[k, 1],
            recv_sem=hr.at[k, 0], device_id={"seq": right}, device_id_type=MESH)
        down = pltpu.make_async_remote_copy(
            src_ref=edge_out.at[k, 0], dst_ref=halo_in.at[k, 1], send_sem=hs.at[k, 0],
            recv_sem=hr.at[k, 1], device_id={"seq": left}, device_id_type=MESH)
        return up, down

    def halo_start(k):
        up, down = halo(k)

        @pl.when(has_right)
        def _():
            up.start()

        @pl.when(has_left)
        def _():
            down.start()

        @pl.when(jnp.logical_not(has_left))
        def _():
            halo_in[k, 0] = jnp.zeros((D, C), BF16)

        @pl.when(jnp.logical_not(has_right))
        def _():
            halo_in[k, 1] = jnp.zeros((D, C), BF16)

    def halo_wait(k):
        up, down = halo(k)

        @pl.when(has_left)
        def _():
            up.wait_recv()

        @pl.when(has_right)
        def _():
            down.wait_recv()

    def halo_drain(k):
        up, down = halo(k)

        @pl.when(has_right)
        def _():
            up.wait_send()

        @pl.when(has_left)
        def _():
            down.wait_send()

    core = h + 1 - 2 * lax.rem(h, 2)
    peers = (h, core, lax.rem(h + 2, haps), lax.rem(core + 2, haps))

    def to_hap(src_of, dst_of, ss, rr, which=(1, 2, 3), to=None):
        out = []
        for d in which:
            t = peers[d if to is None else to]
            c = pltpu.make_async_remote_copy(
                src_ref=src_of(t), dst_ref=dst_of(d), send_sem=ss(d), recv_sem=rr(d),
                device_id={"hap": t}, device_id_type=MESH)
            c.start()
            out.append(c)
        sends.extend(out)
        return out

    def to_seq(src_of, dst_of, ss, rr):
        out = []
        for d in range(1, n):
            t = lax.rem(me + d, n)
            c = pltpu.make_async_remote_copy(
                src_ref=src_of(t), dst_ref=dst_of(d), send_sem=ss(d), recv_sem=rr(d),
                device_id={"seq": t}, device_id_type=MESH)
            c.start()
            out.append(c)
        sends.extend(out)
        return out

    xs[0] = tok[...]
    edge_out[0, 0] = (tok[ds(0), :].astype(F32) * valid[0]).astype(BF16)
    edge_out[0, 1] = (tok[ds(chunks - 1), :].astype(F32) * valid[-1]).astype(BF16)
    if inside:
        pl.semaphore_wait(barrier, n - 1 + haps - 1)
    else:
        @pl.when(has_left)
        def _():
            pl.semaphore_wait(barrier, 1)

        @pl.when(has_right)
        def _():
            pl.semaphore_wait(barrier, 1)
    halo_start(0)
    small_in[2].wait()
    small_in[3].wait()

    def rms(x):
        return lax.rsqrt(jnp.mean(x * x, axis=-1, keepdims=True) + EPS)

    def forward_chunk(l, i):
        pre = (
            taps[0, l : l + 1, :] * npad[l, ds(i), :]
            + taps[1, l : l + 1, :] * npad[l, ds(i + 1), :]
            + taps[2, l : l + 1, :] * npad[l, ds(i + 2), :]
        )
        sq = pre * pre
        th = jnp.tanh(GELU_C * (pre + GELU_A * (sq * pre)))
        half = 0.5 * (1.0 + th)
        hidden = (pre * half).astype(BF16)
        hid[l, ds(i), :] = hidden
        dgelu[l, ds(i), :] = half + 0.5 * pre * (1.0 - th * th) * (GELU_C * (1.0 + 3.0 * GELU_A * sq))

    hT_copies = [None] * LAYERS

    def send_hidden(l):
        hT[l, :, 0:N] = jnp.transpose(hid[l].astype(F32)).astype(BF16)
        if inside:
            hT_copies[l] = to_hap(
                lambda t: hT.at[l, :, pl.ds(0, N)], lambda d: hT.at[l, :, pl.ds(d * N, N)],
                lambda d: hTs.at[l, d], lambda d: hTr.at[l, d], (1, 2))

    def relay_hidden(l):
        if inside:
            hT_copies[l][1].wait_recv()
            hT_copies[l] = [hT_copies[l][0]] + to_hap(
                lambda t: hT.at[l, :, pl.ds(2 * N, N)], lambda d: hT.at[l, :, pl.ds(d * N, N)],
                lambda d: hTs.at[l, d], lambda d: hTr.at[l, d], (3,), 1)

    def start_out(l):
        for c in ag_copies[l]:
            c.wait_recv()
        for q in range(haps):
            pg_out[l, :, q * Q : (q + 1) * Q] = ag[l, q].astype(F32)
        c = pltpu.make_async_copy(pg_out.at[l], pg_hbm.at[l], osem.at[3 + l])
        c.start()
        outs.append(c)

    outs = []
    for l in range(LAYERS):
        gain = gains[l : l + 1, :]
        for i in range(chunks):
            x = xs[l, ds(i), :].astype(F32)
            r = rms(x)
            inv[l, ds(i), :] = r
            npad[l, ds(i + 1), :] = x * r * gain * valid[i]
        for i in inner:
            forward_chunk(l, i)
        halo_wait(l)
        for side, at in ((0, 0), (1, chunks + 1)):
            x = halo_in[l, side].astype(F32)
            npad[l, ds(at), :] = x * rms(x) * gain
        for i in outer:
            forward_chunk(l, i)
        if l + 1 == LAYERS:
            send_hidden(l)
        loads[l].wait()
        proj[l] = jnp.dot(hid[l], w[l], preferred_element_type=F32)
        if l + 1 < LAYERS:
            for i in outer + inner:
                first = proj[l, ds(i), 0:C]
                gate = 0.5 + 0.5 * jnp.tanh(0.5 * proj[l, ds(i), C:PR])
                proj[l, ds(i), C:PR] = gate
                nxt = (xs[l, ds(i), :].astype(F32) + valid[i] * first * gate).astype(BF16)
                xs[l + 1, ds(i), :] = nxt
                if i in outer:
                    edge_out[l + 1, 0 if i == 0 else 1] = (nxt.astype(F32) * valid[i]).astype(BF16)
                if i == outer[-1]:
                    halo_start(l + 1)
        if l + 1 < LAYERS:
            send_hidden(l)

    dq_copies, rs_copies, ag_copies = [[] for _ in range(LAYERS)], [None] * LAYERS, [None] * LAYERS

    def gram(l):
        if not inside:
            pg_out[l] = jnp.dot(hT[l], dp[l], preferred_element_type=F32)
            return
        dq_in[l, 0:N, :] = dp[l, :, pl.ds(pl.multiple_of(h * Q, Q), Q)]
        for c in hT_copies[l] + dq_copies[l]:
            c.wait_recv()
        g = jnp.dot(hT[l], dq_in[l], preferred_element_type=F32)
        gbf[l] = g.astype(BF16).reshape(n, rows, Q)
        rs_copies[l] = to_seq(
            lambda t: gbf.at[l, t], lambda d: rs.at[l, d], lambda d: rss.at[l, d], lambda d: rsr.at[l, d])

    def reduced(l):
        total = gbf[l, me].astype(F32)
        for c in rs_copies[l]:
            c.wait_recv()
        for d in range(1, n):
            total = total + rs[l, d].astype(F32)
        ag[l, h] = total.astype(BF16)
        ag_copies[l] = to_hap(
            lambda t: ag.at[l, h], lambda d: ag.at[l, h], lambda d: ags.at[l, d], lambda d: agr.at[l, d])

    def dproj(l, i):
        last = l == LAYERS - 1
        first = proj[l, ds(i), 0:C]
        gate = proj[l, ds(i), C:PR]
        if last:
            gate = 0.5 + 0.5 * jnp.tanh(0.5 * gate)
        grad = cot[ds(i), :].astype(F32) if last else gcur[ds(i), :]
        bg = valid[i] * grad * gate
        dp[l, ds(i), 0:C] = bg.astype(BF16)
        dp[l, ds(i), C:PR] = (bg * first * (1.0 - gate)).astype(BF16)

    def send_dproj(l, j, start, size):
        if inside:
            dq_copies[l] += to_hap(
                lambda t: dp.at[l, pl.ds(start, size), pl.ds(pl.multiple_of(t * Q, Q), Q)],
                lambda d: dq_in.at[l, pl.ds(d * N + start, size), :],
                lambda d: dqs.at[l, d, j], lambda d: dqr.at[l, d, j])

    def fold(x):
        return jnp.sum(x.reshape(D // 8, 8, C), axis=0)

    small_in[4].wait()
    for l in range(LAYERS - 1):
        relay_hidden(l)
    for i in range(chunks):
        dproj(LAYERS - 1, i)
    send_dproj(LAYERS - 1, 0, 0, N)
    for l in reversed(range(LAYERS)):
        k = 2 * LAYERS - 1 - l
        last = l == LAYERS - 1
        gain = gains[l : l + 1, :]
        if not last:
            gram(l + 1)
        dpad[l, pl.ds(D, N), :] = lax.dot_general(
            dp[l], w[l], (((1,), (1,)), ((), ())), preferred_element_type=F32)
        for i in outer + inner:
            dpre = dpad[l, ds(i + 1), :] * dgelu[l, ds(i), :]
            dpad[l, ds(i + 1), :] = dpre
            if i in outer:
                edge_out[k, 0 if i == 0 else 1] = dpre.astype(BF16)
            if i == outer[-1]:
                halo_start(k)
        g_sum = jnp.zeros((8, C), F32)

        def back_chunk(i, g_sum):
            dn = (
                taps[0, l : l + 1, :] * dpad[l, ds(i + 2), :]
                + taps[1, l : l + 1, :] * dpad[l, ds(i + 1), :]
                + taps[2, l : l + 1, :] * dpad[l, ds(i), :]
            )
            dq = dn * valid[i]
            x = xs[l, ds(i), :].astype(F32)
            r = inv[l, ds(i), :]
            xr = x * r
            g_sum = g_sum + fold(dq * xr)
            dt = dq * gain
            grad = cot[ds(i), :].astype(F32) if last else gcur[ds(i), :]
            new = grad + r * dt - xr * (r * r * jnp.mean(dt * x, axis=-1, keepdims=True))
            if l == 0:
                tg_out[ds(i), :] = new.astype(BF16)
            else:
                gcur[ds(i), :] = new
                dproj(l - 1, i)
            return g_sum

        for i in inner:
            g_sum = back_chunk(i, g_sum)
        if l > 0:
            send_dproj(l - 1, 0, D, N - 2 * D)
        t_sum = [jnp.zeros((8, C), F32) for _ in range(3)]
        for i in range(chunks):
            dpre = dpad[l, ds(i + 1), :]
            for j in range(3):
                t_sum[j] = t_sum[j] + fold(dpre * npad[l, ds(i + j), :])
        for j in range(3):
            smh[h, LAYERS * j + l : LAYERS * j + l + 1, :] = jnp.sum(t_sum[j], axis=0, keepdims=True)
        if l == 0:
            gram(0)
        halo_wait(k)
        if last:
            relay_hidden(l)
        dpad[l, ds(0), :] = halo_in[k, 0].astype(F32)
        dpad[l, ds(chunks + 1), :] = halo_in[k, 1].astype(F32)
        for i in outer:
            g_sum = back_chunk(i, g_sum)
        if l > 0:
            send_dproj(l - 1, 1, 0, D)
            send_dproj(l - 1, 2, N - D, D)
        smh[h, 3 * LAYERS + l : 3 * LAYERS + l + 1, :] = jnp.sum(g_sum, axis=0, keepdims=True)

    c = pltpu.make_async_copy(tg_out, tg_hbm, osem.at[0])
    c.start()
    outs.append(c)
    if inside:
        small = to_hap(lambda t: smh.at[h], lambda d: smh.at[h], lambda d: smhs.at[d], lambda d: smhr.at[d])
        for l in range(1, LAYERS):
            reduced(l)
        for c in small:
            c.wait_recv()
        total = smh[0]
        for q in range(1, haps):
            total = total + smh[q]
        sms[me] = total
        small = to_seq(lambda t: sms.at[me], lambda d: sms.at[me], lambda d: smss.at[d], lambda d: smsr.at[d])
        reduced(0)
        for l in range(1, LAYERS):
            start_out(l)
        for c in small:
            c.wait_recv()
        total = sms[0]
        for q in range(1, n):
            total = total + sms[q]
    else:
        total = smh[h]
        for l in range(LAYERS):
            c = pltpu.make_async_copy(pg_out.at[l], pg_hbm.at[l], osem.at[3 + l])
            c.start()
            outs.append(c)
    for j in range(3):
        tp_out[j] = total[j * LAYERS : (j + 1) * LAYERS, :]
    gn_out[...] = total[3 * LAYERS :, :]
    for c in (pltpu.make_async_copy(tp_out, tp_hbm, osem.at[1]), pltpu.make_async_copy(gn_out, gn_hbm, osem.at[2])):
        c.start()
        outs.append(c)
    if inside:
        start_out(0)
    for k in range(2 * LAYERS):
        halo_drain(k)
    for c in sends:
        c.wait_send()
    for c in outs:
        c.wait()


def finish(a, b, c, d, a_out, b_out, c_out, d_out, sem):
    copies = [
        pltpu.make_async_copy(x, y, sem.at[j])
        for j, (x, y) in enumerate(((b, b_out), (a, a_out), (c, c_out), (d, d_out)))
    ]
    for x in copies:
        x.start()
    for x in copies:
        x.wait()


def shards(n, haps, tokens, cotangent, gaps, conv_taps, norm_gains, projection):
    x = tokens[0]
    N, C = x.shape
    PR = projection.shape[2]
    inside = n > 1 and haps == 4 and C % (16 * n) == 0 and PR % (128 * haps) == 0
    Q, rows = PR // haps, max(C // n, 1)
    L = LAYERS
    wide = haps if inside else 1

    def dma(*shape):
        return pltpu.SemaphoreType.DMA(shape)

    def opt(shape, dtype):
        return pltpu.VMEM(shape if inside else (16, 128), dtype)

    scratch = [
        pltpu.VMEM((N, C), BF16), pltpu.VMEM((N, C), BF16), pltpu.SMEM(gaps.shape, jnp.int32),
        pltpu.VMEM((3, L, C), F32), pltpu.VMEM((L, C), F32), dma(5),
        pltpu.VMEM((L, C, PR), BF16), dma(L),
        pltpu.VMEM((2 * L, 2, D, C), BF16), pltpu.VMEM((2 * L, 2, D, C), BF16), dma(2 * L, 2), dma(2 * L, 2),
        pltpu.VMEM((L, N, C), BF16), pltpu.VMEM((L, N, 1), F32), pltpu.VMEM((L, N + 2 * D, C), F32),
        pltpu.VMEM((L, N, C), F32), pltpu.VMEM((L, N, C), BF16), pltpu.VMEM((L, N, PR), F32),
        pltpu.VMEM((L, N, PR), BF16), pltpu.VMEM((L, N + 2 * D, C), F32), pltpu.VMEM((N, C), F32),
        pltpu.VMEM((L, C, N * wide), BF16), dma(L, haps), dma(L, haps),
        opt((L, N * haps, Q), BF16), dma(L, haps, 3), dma(L, haps, 3),
        opt((L, n, rows, Q), BF16), opt((L, n, rows, Q), BF16), dma(L, n), dma(L, n),
        opt((L, haps, rows, Q), BF16), dma(L, haps), dma(L, haps),
        pltpu.VMEM((haps, 4 * L, C), F32), dma(haps), dma(haps),
        opt((n, 4 * L, C), F32), dma(n), dma(n),
    ]
    hbm = pl.BlockSpec(memory_space=pltpu.HBM)
    outs = [
        jax.ShapeDtypeStruct((N, C), BF16), jax.ShapeDtypeStruct((L, rows if inside else C, PR), F32),
        jax.ShapeDtypeStruct((3, L, C), F32), jax.ShapeDtypeStruct((L, C), F32)]
    scratch = [pltpu.VMEM(o.shape, o.dtype) for o in outs] + [dma(3 + L)] + scratch
    params = dict(vmem_limit_bytes=60 * 1024 * 1024)
    tg, pg, taps, gains = pl.pallas_call(
        functools.partial(kernel, n, haps, inside),
        out_shape=outs,
        in_specs=[hbm] * 6,
        out_specs=[hbm] * 4,
        scratch_shapes=scratch,
        compiler_params=pltpu.CompilerParams(collective_id=0, has_side_effects=True, **params),
    )(x, cotangent[0], gaps, jnp.transpose(conv_taps, (1, 0, 2)), norm_gains, projection)
    if inside:
        tg, pg, taps, gains = pl.pallas_call(
            finish,
            out_shape=outs,
            in_specs=[hbm] * 4,
            out_specs=[hbm] * 4,
            scratch_shapes=[dma(4)],
            compiler_params=pltpu.CompilerParams(**params),
        )(tg, pg, taps, gains)
    else:
        pg = lax.psum(lax.psum_scatter(pg, "seq", scatter_dimension=1, tiled=True), "hap")
        taps, gains = lax.psum((taps, gains), ("seq", "hap"))
    return tg[None], pg, jnp.transpose(taps, (1, 0, 2)), gains


def solution(mesh):
    return jax.shard_map(
        functools.partial(shards, mesh.shape["seq"], mesh.shape["hap"]),
        mesh=mesh,
        in_specs=(P("hap", "seq", None), P("hap", "seq", None), P("seq", None), P(), P(), P()),
        out_specs=(P("hap", "seq", None), P(None, "seq", None), P(), P()),
        check_vma=False,
    )
```

```python
import functools

import jax
import jax.numpy as jnp
from jax import lax
from jax.experimental import pallas as pl
from jax.experimental.pallas import tpu as pltpu
from jax.sharding import PartitionSpec as P

D = 32
LAYERS = 2
EPS = 1e-06
GELU_C = 0.7978845608028654
GELU_A = 0.044715
F32 = jnp.float32
BF16 = jnp.bfloat16
MESH = pl.DeviceIdType.MESH


def kernel(
    n, haps, inside,
    tok_hbm, cot_hbm, gaps_hbm, taps_hbm, gains_hbm, w_hbm,
    tg_hbm, pg_hbm, tp_hbm, gn_hbm,
    tg_out, pg_out, tp_out, gn_out, osem, tok, cot, gaps, taps, gains, isem, w, wsem, edge_out, halo_in, hs, hr, xs, inv, npad, dgelu, hid, proj, dp, dpad, gcur,
    hT, hTs, hTr, dq_in, dqs, dqr, gbf, xr, xrs, xrr, own, zb, zr, zrs, zrr, ag, ags, agr, sml, smh, smhs, smhr, sms, smss, smsr, sma, smas, smar,
):
    me, h = lax.axis_index("seq"), lax.axis_index("hap")
    N, C = tok.shape
    PR = w.shape[2]
    Q, Cq = PR // haps, C // haps
    chunks = N // D
    outer, inner = (0, chunks - 1), tuple(range(1, chunks - 1))
    rows = C // n
    left, right = jnp.maximum(me - 1, 0), jnp.minimum(me + 1, n - 1)
    has_left, has_right = me > 0, me < n - 1
    sends = []

    loads = [pltpu.make_async_copy(w_hbm.at[l], w.at[l], wsem.at[l]) for l in range(LAYERS)]
    small_in = [
        pltpu.make_async_copy(a, b, isem.at[j])
        for j, (a, b) in enumerate(
            ((tok_hbm, tok), (gaps_hbm, gaps), (gains_hbm, gains), (taps_hbm, taps), (cot_hbm, cot)))
    ]
    for c in small_in[:4] + loads + small_in[4:]:
        c.start()

    barrier = pltpu.get_barrier_semaphore()
    if inside:
        for d in range(1, n):
            pl.semaphore_signal(barrier, inc=1, device_id={"seq": lax.rem(me + d, n)}, device_id_type=MESH)
        for d in range(1, haps):
            pl.semaphore_signal(barrier, inc=1, device_id={"hap": lax.rem(h + d, haps)}, device_id_type=MESH)
    else:
        @pl.when(has_left)
        def _():
            pl.semaphore_signal(barrier, inc=1, device_id={"seq": left}, device_id_type=MESH)

        @pl.when(has_right)
        def _():
            pl.semaphore_signal(barrier, inc=1, device_id={"seq": right}, device_id_type=MESH)

    offs = lax.broadcasted_iota(jnp.int32, (D, 1), 0)

    def valid_of(i):
        b = offs + i * D
        return jnp.where((b >= gaps[0, 0]) & (b < gaps[0, 1]), 0.0, 1.0).astype(F32)

    small_in[0].wait()
    small_in[1].wait()
    valid = [valid_of(i) for i in range(chunks)]

    def ds(i):
        return pl.ds(i * D, D)

    def halo(k):
        up = pltpu.make_async_remote_copy(
            src_ref=edge_out.at[k, 1], dst_ref=halo_in.at[k, 0], send_sem=hs.at[k, 1],
            recv_sem=hr.at[k, 0], device_id={"seq": right}, device_id_type=MESH)
        down = pltpu.make_async_remote_copy(
            src_ref=edge_out.at[k, 0], dst_ref=halo_in.at[k, 1], send_sem=hs.at[k, 0],
            recv_sem=hr.at[k, 1], device_id={"seq": left}, device_id_type=MESH)
        return up, down

    def halo_start(k):
        up, down = halo(k)

        @pl.when(has_right)
        def _():
            up.start()

        @pl.when(has_left)
        def _():
            down.start()

        @pl.when(jnp.logical_not(has_left))
        def _():
            halo_in[k, 0] = jnp.zeros((D, C), BF16)

        @pl.when(jnp.logical_not(has_right))
        def _():
            halo_in[k, 1] = jnp.zeros((D, C), BF16)

    def halo_wait(k):
        up, down = halo(k)

        @pl.when(has_left)
        def _():
            up.wait_recv()

        @pl.when(has_right)
        def _():
            down.wait_recv()

    def halo_drain(k):
        up, down = halo(k)

        @pl.when(has_right)
        def _():
            up.wait_send()

        @pl.when(has_left)
        def _():
            down.wait_send()

    core = h + 1 - 2 * lax.rem(h, 2)
    peers = (h, core, lax.rem(h + 2, haps), lax.rem(core + 2, haps))

    def to_hap(src_of, dst_of, ss, rr, which=(1, 2, 3), to=None):
        out = []
        for d in which:
            t = peers[d if to is None else to]
            c = pltpu.make_async_remote_copy(
                src_ref=src_of(t), dst_ref=dst_of(d), send_sem=ss(d), recv_sem=rr(d),
                device_id={"hap": t}, device_id_type=MESH)
            c.start()
            out.append(c)
        sends.extend(out)
        return out

    def to_seq(src_of, dst_of, ss, rr):
        out = []
        for d in range(1, n):
            t = lax.rem(me + d, n)
            c = pltpu.make_async_remote_copy(
                src_ref=src_of(t), dst_ref=dst_of(d), send_sem=ss(d), recv_sem=rr(d),
                device_id={"seq": t}, device_id_type=MESH)
            c.start()
            out.append(c)
        sends.extend(out)
        return out

    xs[0] = tok[...]
    edge_out[0, 0] = (tok[ds(0), :].astype(F32) * valid[0]).astype(BF16)
    edge_out[0, 1] = (tok[ds(chunks - 1), :].astype(F32) * valid[-1]).astype(BF16)
    if inside:
        pl.semaphore_wait(barrier, n - 1 + haps - 1)
    else:
        @pl.when(has_left)
        def _():
            pl.semaphore_wait(barrier, 1)

        @pl.when(has_right)
        def _():
            pl.semaphore_wait(barrier, 1)
    halo_start(0)
    small_in[2].wait()
    small_in[3].wait()

    def rms(x):
        return lax.rsqrt(jnp.mean(x * x, axis=-1, keepdims=True) + EPS)

    def forward_chunk(l, i):
        pre = (
            taps[0, l : l + 1, :] * npad[l, ds(i), :]
            + taps[1, l : l + 1, :] * npad[l, ds(i + 1), :]
            + taps[2, l : l + 1, :] * npad[l, ds(i + 2), :]
        )
        sq = pre * pre
        th = jnp.tanh(GELU_C * (pre + GELU_A * (sq * pre)))
        half = 0.5 * (1.0 + th)
        hidden = (pre * half).astype(BF16)
        hid[l, ds(i), :] = hidden
        dgelu[l, ds(i), :] = half + 0.5 * pre * (1.0 - th * th) * (GELU_C * (1.0 + 3.0 * GELU_A * sq))

    hT_copies = [None] * LAYERS

    def send_hidden(l):
        hT[l, :, 0:N] = jnp.transpose(hid[l].astype(F32)).astype(BF16)
        if inside:
            hT_copies[l] = to_hap(
                lambda t: hT.at[l, :, pl.ds(0, N)], lambda d: hT.at[l, :, pl.ds(d * N, N)],
                lambda d: hTs.at[l, d], lambda d: hTr.at[l, d], (1, 2))

    def relay_hidden(l):
        if inside:
            hT_copies[l][1].wait_recv()
            hT_copies[l] = [hT_copies[l][0]] + to_hap(
                lambda t: hT.at[l, :, pl.ds(2 * N, N)], lambda d: hT.at[l, :, pl.ds(d * N, N)],
                lambda d: hTs.at[l, d], lambda d: hTr.at[l, d], (3,), 1)

    def start_out(l):
        for c in ag_copies[l]:
            c.wait_recv()
        for q in range(haps):
            pg_out[l, :, q * Q : (q + 1) * Q] = ag[l, q].astype(F32)
        c = pltpu.make_async_copy(pg_out.at[l], pg_hbm.at[l], osem.at[3 + l])
        c.start()
        outs.append(c)

    outs = []
    for l in range(LAYERS):
        gain = gains[l : l + 1, :]
        for i in range(chunks):
            x = xs[l, ds(i), :].astype(F32)
            r = rms(x)
            inv[l, ds(i), :] = r
            npad[l, ds(i + 1), :] = x * r * gain * valid[i]
        for i in inner:
            forward_chunk(l, i)
        halo_wait(l)
        for side, at in ((0, 0), (1, chunks + 1)):
            x = halo_in[l, side].astype(F32)
            npad[l, ds(at), :] = x * rms(x) * gain
        for i in outer:
            forward_chunk(l, i)
        if l + 1 == LAYERS:
            send_hidden(l)
        loads[l].wait()
        proj[l] = jnp.dot(hid[l], w[l], preferred_element_type=F32)
        if l + 1 < LAYERS:
            for i in outer + inner:
                first = proj[l, ds(i), 0:C]
                gate = 0.5 + 0.5 * jnp.tanh(0.5 * proj[l, ds(i), C:PR])
                proj[l, ds(i), C:PR] = gate
                nxt = (xs[l, ds(i), :].astype(F32) + valid[i] * first * gate).astype(BF16)
                xs[l + 1, ds(i), :] = nxt
                if i in outer:
                    edge_out[l + 1, 0 if i == 0 else 1] = (nxt.astype(F32) * valid[i]).astype(BF16)
                if i == outer[-1]:
                    halo_start(l + 1)
        if l + 1 < LAYERS:
            send_hidden(l)

    dq_copies, x_copies, z_copies, ag_copies = [[[] for _ in range(LAYERS)] for _ in range(4)]
    nz = n // 2
    z, x = me // 2, lax.rem(me, 2)
    order = [nz // 2] + [j for j in range(1, nz) if j != nz // 2] + [0]

    def gram(l):
        if not inside:
            pg_out[l] = jnp.dot(hT[l], dp[l], preferred_element_type=F32)
            return
        dq_in[l, 0:N, :] = dp[l, :, pl.ds(pl.multiple_of(h * Q, Q), Q)]
        for c in hT_copies[l] + dq_copies[l]:
            c.wait_recv()
        g = jnp.dot(hT[l], dq_in[l], preferred_element_type=F32)
        gbf[l] = g.astype(BF16).reshape(n, rows, Q)
        for j in order:
            c = pltpu.make_async_remote_copy(
                src_ref=gbf.at[l, 2 * lax.rem(z + j, nz) + 1 - x], dst_ref=xr.at[l, j],
                send_sem=xrs.at[l, j], recv_sem=xrr.at[l, j],
                device_id={"seq": 2 * z + 1 - x}, device_id_type=MESH)
            c.start()
            x_copies[l].append(c)
        sends.extend(x_copies[l])

    def forward(l):
        for j, c in zip(order, x_copies[l]):
            t = 2 * lax.rem(z + j, nz) + x
            c.wait_recv()
            total = gbf[l, t].astype(F32) + xr[l, j].astype(F32)
            if j == 0:
                own[l] = total
                continue
            zb[l, j] = total.astype(BF16)
            c = pltpu.make_async_remote_copy(
                src_ref=zb.at[l, j], dst_ref=zr.at[l, j], send_sem=zrs.at[l, j], recv_sem=zrr.at[l, j],
                device_id={"seq": t}, device_id_type=MESH)
            c.start()
            z_copies[l].append((j, c))
            sends.append(c)

    def reduced(l):
        total = own[l]
        for j, c in z_copies[l]:
            c.wait_recv()
            total = total + zr[l, j].astype(F32)
        ag[l, h] = total.astype(BF16)
        ag_copies[l] = to_hap(
            lambda t: ag.at[l, h], lambda d: ag.at[l, h], lambda d: ags.at[l, d], lambda d: agr.at[l, d])

    def dproj(l, i):
        last = l == LAYERS - 1
        first = proj[l, ds(i), 0:C]
        gate = proj[l, ds(i), C:PR]
        if last:
            gate = 0.5 + 0.5 * jnp.tanh(0.5 * gate)
        grad = cot[ds(i), :].astype(F32) if last else gcur[ds(i), :]
        bg = valid[i] * grad * gate
        dp[l, ds(i), 0:C] = bg.astype(BF16)
        dp[l, ds(i), C:PR] = (bg * first * (1.0 - gate)).astype(BF16)

    def send_dproj(l, j, start, size):
        if inside:
            dq_copies[l] += to_hap(
                lambda t: dp.at[l, pl.ds(start, size), pl.ds(pl.multiple_of(t * Q, Q), Q)],
                lambda d: dq_in.at[l, pl.ds(d * N + start, size), :],
                lambda d: dqs.at[l, d, j], lambda d: dqr.at[l, d, j])

    def fold(x):
        return jnp.sum(x.reshape(D // 8, 8, C), axis=0)

    small_in[4].wait()
    for l in range(LAYERS - 1):
        relay_hidden(l)
    for i in range(chunks):
        dproj(LAYERS - 1, i)
    send_dproj(LAYERS - 1, 0, 0, N)
    for l in reversed(range(LAYERS)):
        k = 2 * LAYERS - 1 - l
        last = l == LAYERS - 1
        gain = gains[l : l + 1, :]
        if not last:
            gram(l + 1)
        dpad[l, pl.ds(D, N), :] = lax.dot_general(
            dp[l], w[l], (((1,), (1,)), ((), ())), preferred_element_type=F32)
        for i in outer + inner:
            dpre = dpad[l, ds(i + 1), :] * dgelu[l, ds(i), :]
            dpad[l, ds(i + 1), :] = dpre
            if i in outer:
                edge_out[k, 0 if i == 0 else 1] = dpre.astype(BF16)
            if i == outer[-1]:
                halo_start(k)
        g_sum = jnp.zeros((8, C), F32)

        def back_chunk(i, g_sum):
            dn = (
                taps[0, l : l + 1, :] * dpad[l, ds(i + 2), :]
                + taps[1, l : l + 1, :] * dpad[l, ds(i + 1), :]
                + taps[2, l : l + 1, :] * dpad[l, ds(i), :]
            )
            dq = dn * valid[i]
            x = xs[l, ds(i), :].astype(F32)
            r = inv[l, ds(i), :]
            xr = x * r
            g_sum = g_sum + fold(dq * xr)
            dt = dq * gain
            grad = cot[ds(i), :].astype(F32) if last else gcur[ds(i), :]
            new = grad + r * dt - xr * (r * r * jnp.mean(dt * x, axis=-1, keepdims=True))
            if l == 0:
                tg_out[ds(i), :] = new.astype(BF16)
            else:
                gcur[ds(i), :] = new
                dproj(l - 1, i)
            return g_sum

        for i in inner:
            g_sum = back_chunk(i, g_sum)
        if l > 0:
            send_dproj(l - 1, 0, D, N - 2 * D)
        t_sum = [jnp.zeros((8, C), F32) for _ in range(3)]
        for i in range(chunks):
            dpre = dpad[l, ds(i + 1), :]
            for j in range(3):
                t_sum[j] = t_sum[j] + fold(dpre * npad[l, ds(i + j), :])
        for j in range(3):
            sml[LAYERS * j + l : LAYERS * j + l + 1, :] = jnp.sum(t_sum[j], axis=0, keepdims=True)
        if l == 0:
            if inside:
                for m in range(1, LAYERS):
                    forward(m)
            gram(0)
        halo_wait(k)
        if last:
            relay_hidden(l)
        dpad[l, ds(0), :] = halo_in[k, 0].astype(F32)
        dpad[l, ds(chunks + 1), :] = halo_in[k, 1].astype(F32)
        for i in outer:
            g_sum = back_chunk(i, g_sum)
        if l > 0:
            send_dproj(l - 1, 1, 0, D)
            send_dproj(l - 1, 2, N - D, D)
        sml[3 * LAYERS + l : 3 * LAYERS + l + 1, :] = jnp.sum(g_sum, axis=0, keepdims=True)

    c = pltpu.make_async_copy(tg_out, tg_hbm, osem.at[0])
    c.start()
    outs.append(c)
    if inside:
        def quarter(t):
            return pl.ds(pl.multiple_of(t * Cq, Cq), Cq)

        smh[h] = sml[:, quarter(h)]
        small = to_hap(
            lambda t: sml.at[:, quarter(t)], lambda d: smh.at[h], lambda d: smhs.at[d], lambda d: smhr.at[d])
        forward(0)
        for c in small:
            c.wait_recv()
        total = smh[0]
        for q in range(1, haps):
            total = total + smh[q]
        sms[me] = total
        small = to_seq(lambda t: sms.at[me], lambda d: sms.at[me], lambda d: smss.at[d], lambda d: smsr.at[d])
        for l in range(1, LAYERS):
            reduced(l)
        reduced(0)
        for l in range(1, LAYERS):
            start_out(l)
        for c in small:
            c.wait_recv()
        total = sms[0]
        for q in range(1, n):
            total = total + sms[q]
        sma[h] = total
        small = to_hap(lambda t: sma.at[h], lambda d: sma.at[h], lambda d: smas.at[d], lambda d: smar.at[d])
        for c in small:
            c.wait_recv()
        parts = [(q * Cq, Cq, sma[q]) for q in range(haps)]
    else:
        parts = [(0, C, sml[...])]
        for l in range(LAYERS):
            c = pltpu.make_async_copy(pg_out.at[l], pg_hbm.at[l], osem.at[3 + l])
            c.start()
            outs.append(c)
    for at, size, total in parts:
        for j in range(3):
            tp_out[j, :, at : at + size] = total[j * LAYERS : (j + 1) * LAYERS, :]
        gn_out[:, at : at + size] = total[3 * LAYERS :, :]
    for c in (pltpu.make_async_copy(tp_out, tp_hbm, osem.at[1]), pltpu.make_async_copy(gn_out, gn_hbm, osem.at[2])):
        c.start()
        outs.append(c)
    if inside:
        start_out(0)
    for k in range(2 * LAYERS):
        halo_drain(k)
    for c in sends:
        c.wait_send()
    for c in outs:
        c.wait()


def finish(a, b, c, d, a_out, b_out, c_out, d_out, a_in, b_in, c_in, d_in, sem):
    refs = ((b, b_in, b_out), (a, a_in, a_out), (c, c_in, c_out), (d, d_in, d_out))
    loads = [pltpu.make_async_copy(x, y, sem.at[0, j]) for j, (x, y, _) in enumerate(refs)]
    stores = [pltpu.make_async_copy(y, z, sem.at[1, j]) for j, (_, y, z) in enumerate(refs)]
    for x in loads:
        x.start()
    for x, y in zip(loads, stores):
        x.wait()
        y.start()
    for y in stores:
        y.wait()


def shards(n, haps, tokens, cotangent, gaps, conv_taps, norm_gains, projection):
    x = tokens[0]
    N, C = x.shape
    PR = projection.shape[2]
    inside = n > 2 and n % 2 == 0 and haps == 4 and C % (16 * n) == 0 and C % (128 * haps) == 0
    Cq, nz = C // haps, max(n // 2, 1)
    Q, rows = PR // haps, max(C // n, 1)
    L = LAYERS
    wide = haps if inside else 1

    def dma(*shape):
        return pltpu.SemaphoreType.DMA(shape)

    def opt(shape, dtype):
        return pltpu.VMEM(shape if inside else (16, 128), dtype)

    scratch = [
        pltpu.VMEM((N, C), BF16), pltpu.VMEM((N, C), BF16), pltpu.SMEM(gaps.shape, jnp.int32),
        pltpu.VMEM((3, L, C), F32), pltpu.VMEM((L, C), F32), dma(5),
        pltpu.VMEM((L, C, PR), BF16), dma(L),
        pltpu.VMEM((2 * L, 2, D, C), BF16), pltpu.VMEM((2 * L, 2, D, C), BF16), dma(2 * L, 2), dma(2 * L, 2),
        pltpu.VMEM((L, N, C), BF16), pltpu.VMEM((L, N, 1), F32), pltpu.VMEM((L, N + 2 * D, C), F32),
        pltpu.VMEM((L, N, C), F32), pltpu.VMEM((L, N, C), BF16), pltpu.VMEM((L, N, PR), F32),
        pltpu.VMEM((L, N, PR), BF16), pltpu.VMEM((L, N + 2 * D, C), F32), pltpu.VMEM((N, C), F32),
        pltpu.VMEM((L, C, N * wide), BF16), dma(L, haps), dma(L, haps),
        opt((L, N * haps, Q), BF16), dma(L, haps, 3), dma(L, haps, 3),
        opt((L, n, rows, Q), BF16), opt((L, nz, rows, Q), BF16), dma(L, nz), dma(L, nz),
        opt((L, rows, Q), F32), opt((L, nz, rows, Q), BF16), opt((L, nz, rows, Q), BF16), dma(L, nz), dma(L, nz),
        opt((L, haps, rows, Q), BF16), dma(L, haps), dma(L, haps),
        pltpu.VMEM((4 * L, C), F32), opt((haps, 4 * L, Cq), F32), dma(haps), dma(haps),
        opt((n, 4 * L, Cq), F32), dma(n), dma(n), opt((haps, 4 * L, Cq), F32), dma(haps), dma(haps),
    ]
    hbm = pl.BlockSpec(memory_space=pltpu.HBM)
    outs = [
        jax.ShapeDtypeStruct((N, C), BF16), jax.ShapeDtypeStruct((L, rows if inside else C, PR), F32),
        jax.ShapeDtypeStruct((3, L, C), F32), jax.ShapeDtypeStruct((L, C), F32)]
    scratch = [pltpu.VMEM(o.shape, o.dtype) for o in outs] + [dma(3 + L)] + scratch
    params = dict(vmem_limit_bytes=60 * 1024 * 1024)
    tg, pg, taps, gains = pl.pallas_call(
        functools.partial(kernel, n, haps, inside),
        out_shape=outs,
        in_specs=[hbm] * 6,
        out_specs=[hbm] * 4,
        scratch_shapes=scratch,
        compiler_params=pltpu.CompilerParams(collective_id=0, has_side_effects=True, **params),
    )(x, cotangent[0], gaps, jnp.transpose(conv_taps, (1, 0, 2)), norm_gains, projection)
    if inside:
        tg, pg, taps, gains = pl.pallas_call(
            finish,
            out_shape=outs,
            in_specs=[hbm] * 4,
            out_specs=[hbm] * 4,
            scratch_shapes=[pltpu.VMEM(o.shape, o.dtype) for o in outs] + [dma(2, 4)],
            compiler_params=pltpu.CompilerParams(**params),
        )(tg, pg, taps, gains)
    else:
        pg = lax.psum(lax.psum_scatter(pg, "seq", scatter_dimension=1, tiled=True), "hap")
        taps, gains = lax.psum((taps, gains), ("seq", "hap"))
    return tg[None], pg, jnp.transpose(taps, (1, 0, 2)), gains


def solution(mesh):
    return jax.shard_map(
        functools.partial(shards, mesh.shape["seq"], mesh.shape["hap"]),
        mesh=mesh,
        in_specs=(P("hap", "seq", None), P("hap", "seq", None), P("seq", None), P(), P(), P()),
        out_specs=(P("hap", "seq", None), P(None, "seq", None), P(), P()),
        check_vma=False,
    )
```

```python
import functools

import jax
import jax.numpy as jnp
from jax import lax
from jax.experimental import pallas as pl
from jax.experimental.pallas import tpu as pltpu
from jax.sharding import PartitionSpec as P

D = 32
LAYERS = 2
EPS = 1e-06
GELU_C = 0.7978845608028654
GELU_A = 0.044715
F32 = jnp.float32
BF16 = jnp.bfloat16
MESH = pl.DeviceIdType.MESH


def kernel(
    n, haps, inside,
    tok_hbm, cot_hbm, gaps_hbm, taps_hbm, gains_hbm, w_hbm,
    tg_hbm, pg_hbm, sm_hbm,
    tg_out, pg_out, osem, tok, cot, gaps, taps, gains, isem, w, wsem, edge_out, halo_in, hs, hr, xs, inv, npad, dgelu, hid, proj, dp, dpad, gcur,
    hT, hTs, hTr, dq_in, dqs, dqr, gbf, xr, xrs, xrr, own, zb, zr, zrs, zrr, ag, ags, agr, sml, smh, smhs, smhr, sms, smss, smsr, sma, smas, smar,
):
    me, h = lax.axis_index("seq"), lax.axis_index("hap")
    N, C = tok.shape
    PR = w.shape[2]
    Q, Cq = PR // haps, C // haps
    chunks = N // D
    outer, inner = (0, chunks - 1), tuple(range(1, chunks - 1))
    rows = C // n
    left, right = jnp.maximum(me - 1, 0), jnp.minimum(me + 1, n - 1)
    has_left, has_right = me > 0, me < n - 1
    sends = []

    loads = [pltpu.make_async_copy(w_hbm.at[l], w.at[l], wsem.at[l]) for l in range(LAYERS)]
    small_in = [
        pltpu.make_async_copy(a, b, isem.at[j])
        for j, (a, b) in enumerate(
            ((tok_hbm, tok), (gaps_hbm, gaps), (gains_hbm, gains), (taps_hbm, taps), (cot_hbm, cot)))
    ]
    for c in small_in[:4] + loads + small_in[4:]:
        c.start()

    barrier = pltpu.get_barrier_semaphore()
    if inside:
        for d in range(1, n):
            pl.semaphore_signal(barrier, inc=1, device_id={"seq": lax.rem(me + d, n)}, device_id_type=MESH)
        for d in range(1, haps):
            pl.semaphore_signal(barrier, inc=1, device_id={"hap": lax.rem(h + d, haps)}, device_id_type=MESH)
    else:
        @pl.when(has_left)
        def _():
            pl.semaphore_signal(barrier, inc=1, device_id={"seq": left}, device_id_type=MESH)

        @pl.when(has_right)
        def _():
            pl.semaphore_signal(barrier, inc=1, device_id={"seq": right}, device_id_type=MESH)

    offs = lax.broadcasted_iota(jnp.int32, (D, 1), 0)

    def valid_of(i):
        b = offs + i * D
        return jnp.where((b >= gaps[0, 0]) & (b < gaps[0, 1]), 0.0, 1.0).astype(F32)

    small_in[0].wait()
    small_in[1].wait()
    valid = [valid_of(i) for i in range(chunks)]

    def ds(i):
        return pl.ds(i * D, D)

    def halo(k):
        up = pltpu.make_async_remote_copy(
            src_ref=edge_out.at[k, 1], dst_ref=halo_in.at[k, 0], send_sem=hs.at[k, 1],
            recv_sem=hr.at[k, 0], device_id={"seq": right}, device_id_type=MESH)
        down = pltpu.make_async_remote_copy(
            src_ref=edge_out.at[k, 0], dst_ref=halo_in.at[k, 1], send_sem=hs.at[k, 0],
            recv_sem=hr.at[k, 1], device_id={"seq": left}, device_id_type=MESH)
        return up, down

    def halo_start(k):
        up, down = halo(k)

        @pl.when(has_right)
        def _():
            up.start()

        @pl.when(has_left)
        def _():
            down.start()

        @pl.when(jnp.logical_not(has_left))
        def _():
            halo_in[k, 0] = jnp.zeros((D, C), BF16)

        @pl.when(jnp.logical_not(has_right))
        def _():
            halo_in[k, 1] = jnp.zeros((D, C), BF16)

    def halo_wait(k):
        up, down = halo(k)

        @pl.when(has_left)
        def _():
            up.wait_recv()

        @pl.when(has_right)
        def _():
            down.wait_recv()

    def halo_drain(k):
        up, down = halo(k)

        @pl.when(has_right)
        def _():
            up.wait_send()

        @pl.when(has_left)
        def _():
            down.wait_send()

    core = h + 1 - 2 * lax.rem(h, 2)
    peers = (h, core, lax.rem(h + 2, haps), lax.rem(core + 2, haps))

    def to_hap(src_of, dst_of, ss, rr, which=(1, 2, 3), to=None):
        out = []
        for d in which:
            t = peers[d if to is None else to]
            c = pltpu.make_async_remote_copy(
                src_ref=src_of(t), dst_ref=dst_of(d), send_sem=ss(d), recv_sem=rr(d),
                device_id={"hap": t}, device_id_type=MESH)
            c.start()
            out.append(c)
        sends.extend(out)
        return out

    def to_seq(src_of, dst_of, ss, rr):
        out = []
        for d in range(1, n):
            t = lax.rem(me + d, n)
            c = pltpu.make_async_remote_copy(
                src_ref=src_of(t), dst_ref=dst_of(d), send_sem=ss(d), recv_sem=rr(d),
                device_id={"seq": t}, device_id_type=MESH)
            c.start()
            out.append(c)
        sends.extend(out)
        return out

    xs[0] = tok[...]
    edge_out[0, 0] = (tok[ds(0), :].astype(F32) * valid[0]).astype(BF16)
    edge_out[0, 1] = (tok[ds(chunks - 1), :].astype(F32) * valid[-1]).astype(BF16)
    if inside:
        pl.semaphore_wait(barrier, n - 1 + haps - 1)
    else:
        @pl.when(has_left)
        def _():
            pl.semaphore_wait(barrier, 1)

        @pl.when(has_right)
        def _():
            pl.semaphore_wait(barrier, 1)
    halo_start(0)
    small_in[2].wait()
    small_in[3].wait()

    def rms(x):
        return lax.rsqrt(jnp.mean(x * x, axis=-1, keepdims=True) + EPS)

    def forward_chunk(l, i):
        pre = (
            taps[0, l : l + 1, :] * npad[l, ds(i), :]
            + taps[1, l : l + 1, :] * npad[l, ds(i + 1), :]
            + taps[2, l : l + 1, :] * npad[l, ds(i + 2), :]
        )
        sq = pre * pre
        th = jnp.tanh(GELU_C * (pre + GELU_A * (sq * pre)))
        half = 0.5 * (1.0 + th)
        hidden = (pre * half).astype(BF16)
        hid[l, ds(i), :] = hidden
        dgelu[l, ds(i), :] = half + 0.5 * pre * (1.0 - th * th) * (GELU_C * (1.0 + 3.0 * GELU_A * sq))

    hT_copies = [None] * LAYERS

    def send_hidden(l):
        hT[l, 0] = jnp.transpose(hid[l].astype(F32)).astype(BF16)
        if inside:
            hT_copies[l] = to_hap(
                lambda t: hT.at[l, 0], lambda d: hT.at[l, d],
                lambda d: hTs.at[l, d], lambda d: hTr.at[l, d], (1, 2))

    def relay_hidden(l):
        if inside:
            hT_copies[l][1].wait_recv()
            hT_copies[l] = [hT_copies[l][0]] + to_hap(
                lambda t: hT.at[l, 2], lambda d: hT.at[l, d],
                lambda d: hTs.at[l, d], lambda d: hTr.at[l, d], (3,), 1)

    def norm_chunk(l, i):
        v = xs[l, ds(i), :].astype(F32)
        r = rms(v)
        inv[l, ds(i), :] = r
        npad[l, ds(i + 1), :] = v * r * gains[l : l + 1, :] * valid[i]

    def project(l, which):
        y = jnp.dot(
            jnp.concatenate([hid[l, ds(i), :] for i in which], axis=0), w[l], preferred_element_type=F32)
        for j, i in enumerate(which):
            first = y[j * D : (j + 1) * D, 0:C]
            gate = 0.5 + 0.5 * jnp.tanh(0.5 * y[j * D : (j + 1) * D, C:PR])
            proj[l, ds(i), 0:C] = first
            proj[l, ds(i), C:PR] = gate
            if l + 1 < LAYERS:
                nxt = (xs[l, ds(i), :].astype(F32) + valid[i] * first * gate).astype(BF16)
                xs[l + 1, ds(i), :] = nxt
                if i in outer:
                    edge_out[l + 1, 0 if i == 0 else 1] = (nxt.astype(F32) * valid[i]).astype(BF16)

    def dproj(l, i):
        first = proj[l, ds(i), 0:C]
        gate = proj[l, ds(i), C:PR]
        grad = cot[ds(i), :].astype(F32) if l == LAYERS - 1 else gcur[ds(i), :]
        bg = valid[i] * grad * gate
        both = jnp.concatenate([bg, bg * first * (1.0 - gate)], axis=1).astype(BF16)
        for q in range(haps):
            dp[l, q, ds(i), :] = both[:, q * Q : (q + 1) * Q]

    def send_dproj(l, which):
        if not inside:
            return
        blocks = [(0, D, N - 2 * D)] if which == inner else [(1, 0, D), (2, N - D, D)]
        for j, start, size in blocks:
            dq_copies[l] += to_hap(
                lambda t: dp.at[l, t, pl.ds(start, size), :],
                lambda d: dq_in.at[l, pl.ds(d * N + start, size), :],
                lambda d: dqs.at[l, d, j], lambda d: dqr.at[l, d, j])

    def dconv(l, which):
        y = lax.dot_general(
            jnp.concatenate(
                [jnp.concatenate([dp[l, q, ds(i), :] for q in range(haps)], axis=1) for i in which], axis=0),
            w[l], (((1,), (1,)), ((), ())), preferred_element_type=F32)
        for j, i in enumerate(which):
            dpre = y[j * D : (j + 1) * D, :] * dgelu[l, ds(i), :]
            dpad[l, ds(i + 1), :] = dpre
            if i in outer:
                edge_out[2 * LAYERS - 1 - l, 0 if i == 0 else 1] = dpre.astype(BF16)

    def fold(v):
        return jnp.sum(v.reshape(D // 8, 8, C), axis=0)

    outs = []
    dq_copies, x_copies, z_copies, ag_copies = [[[] for _ in range(LAYERS)] for _ in range(4)]
    nz = n // 2
    z, x = me // 2, lax.rem(me, 2)
    order = [nz // 2] + [j for j in range(1, nz) if j != nz // 2] + [0]

    for l in range(LAYERS):
        last = l == LAYERS - 1
        for i in range(chunks):
            norm_chunk(l, i)
        for i in inner:
            forward_chunk(l, i)
        loads[l].wait()
        project(l, inner)
        if last:
            small_in[4].wait()
            for i in inner:
                dproj(l, i)
            send_dproj(l, inner)
            dconv(l, inner)
        halo_wait(l)
        for side, at in ((0, 0), (1, chunks + 1)):
            v = halo_in[l, side].astype(F32)
            npad[l, ds(at), :] = v * rms(v) * gains[l : l + 1, :]
        for i in outer:
            forward_chunk(l, i)
        if last:
            send_hidden(l)
        project(l, outer)
        if last:
            for i in outer:
                dproj(l, i)
            dconv(l, outer)
            halo_start(l + 1)
            send_dproj(l, outer)
        else:
            halo_start(l + 1)
            send_hidden(l)

    def gram(l):
        if not inside:
            pg_out[l] = jnp.dot(
                hT[l, 0], jnp.concatenate([dp[l, q] for q in range(haps)], axis=1), preferred_element_type=F32)
            return
        dq_in[l, 0:N, :] = dp[l, h]
        for c in hT_copies[l] + dq_copies[l]:
            c.wait_recv()
        g = jnp.dot(
            jnp.concatenate([hT[l, d] for d in range(haps)], axis=1), dq_in[l], preferred_element_type=F32)
        gbf[l] = g.astype(BF16).reshape(n, rows, Q)
        for j in order:
            c = pltpu.make_async_remote_copy(
                src_ref=gbf.at[l, 2 * lax.rem(z + j, nz) + 1 - x], dst_ref=xr.at[l, j],
                send_sem=xrs.at[l, j], recv_sem=xrr.at[l, j],
                device_id={"seq": 2 * z + 1 - x}, device_id_type=MESH)
            c.start()
            x_copies[l].append(c)
        sends.extend(x_copies[l])

    def forward(l):
        for j, c in zip(order, x_copies[l]):
            t = 2 * lax.rem(z + j, nz) + x
            c.wait_recv()
            total = gbf[l, t].astype(F32) + xr[l, j].astype(F32)
            if j == 0:
                own[l] = total
                continue
            zb[l, j] = total.astype(BF16)
            c = pltpu.make_async_remote_copy(
                src_ref=zb.at[l, j], dst_ref=zr.at[l, j], send_sem=zrs.at[l, j], recv_sem=zrr.at[l, j],
                device_id={"seq": t}, device_id_type=MESH)
            c.start()
            z_copies[l].append((j, c))
            sends.append(c)

    def reduced(l):
        total = own[l]
        for j, c in z_copies[l]:
            c.wait_recv()
            total = total + zr[l, j].astype(F32)
        ag[l] = total.astype(BF16)
        ag_copies[l] = to_hap(
            lambda t: ag.at[l], lambda d: pg_hbm.at[l, h], lambda d: ags.at[l, d], lambda d: agr.at[l, d])
        c = pltpu.make_async_copy(ag.at[l], pg_hbm.at[l, h], osem.at[2 + l])
        c.start()
        outs.append(c)

    for l in range(LAYERS - 1):
        relay_hidden(l)
    for l in reversed(range(LAYERS)):
        k = 2 * LAYERS - 1 - l
        last = l == LAYERS - 1
        g_sum = jnp.zeros((8, C), F32)

        def back_chunk(i, g_sum):
            dn = (
                taps[0, l : l + 1, :] * dpad[l, ds(i + 2), :]
                + taps[1, l : l + 1, :] * dpad[l, ds(i + 1), :]
                + taps[2, l : l + 1, :] * dpad[l, ds(i), :]
            )
            dq = dn * valid[i]
            v = xs[l, ds(i), :].astype(F32)
            r = inv[l, ds(i), :]
            vr = v * r
            g_sum = g_sum + fold(dq * vr)
            dt = dq * gains[l : l + 1, :]
            grad = cot[ds(i), :].astype(F32) if last else gcur[ds(i), :]
            new = grad + r * dt - vr * (r * r * jnp.mean(dt * v, axis=-1, keepdims=True))
            if l == 0:
                tg_out[ds(i), :] = new.astype(BF16)
            else:
                gcur[ds(i), :] = new
                dproj(l - 1, i)
            return g_sum

        for i in inner:
            g_sum = back_chunk(i, g_sum)
        if l > 0:
            send_dproj(l - 1, inner)
            dconv(l - 1, inner)
        t_sum = [jnp.zeros((8, C), F32) for _ in range(3)]
        for i in range(chunks):
            dpre = dpad[l, ds(i + 1), :]
            for j in range(3):
                t_sum[j] = t_sum[j] + fold(dpre * npad[l, ds(i + j), :])
        for j in range(3):
            sml[LAYERS * j + l : LAYERS * j + l + 1, :] = jnp.sum(t_sum[j], axis=0, keepdims=True)
        if l == 0:
            if inside:
                for m in range(1, LAYERS):
                    forward(m)
            gram(0)
        halo_wait(k)
        dpad[l, ds(0), :] = halo_in[k, 0].astype(F32)
        dpad[l, ds(chunks + 1), :] = halo_in[k, 1].astype(F32)
        for i in outer:
            g_sum = back_chunk(i, g_sum)
        if l > 0:
            send_dproj(l - 1, outer)
            relay_hidden(l)
            dconv(l - 1, outer)
            halo_start(k + 1)
            gram(l)
        sml[3 * LAYERS + l : 3 * LAYERS + l + 1, :] = jnp.sum(g_sum, axis=0, keepdims=True)

    c = pltpu.make_async_copy(tg_out, tg_hbm, osem.at[0])
    c.start()
    outs.append(c)
    if inside:
        def quarter(t):
            return pl.ds(pl.multiple_of(t * Cq, Cq), Cq)

        smh[h] = sml[:, quarter(h)]
        small = to_hap(
            lambda t: sml.at[:, quarter(t)], lambda d: smh.at[h], lambda d: smhs.at[d], lambda d: smhr.at[d])
        forward(0)
        for c in small:
            c.wait_recv()
        total = smh[0]
        for q in range(1, haps):
            total = total + smh[q]
        sms[me] = total
        small = to_seq(lambda t: sms.at[me], lambda d: sms.at[me], lambda d: smss.at[d], lambda d: smsr.at[d])
        for l in range(1, LAYERS):
            reduced(l)
        reduced(0)
        for c in small:
            c.wait_recv()
        total = sms[0]
        for q in range(1, n):
            total = total + sms[q]
        sma[...] = total
        small = to_hap(lambda t: sma, lambda d: sm_hbm.at[h], lambda d: smas.at[d], lambda d: smar.at[d])
        c = pltpu.make_async_copy(sma, sm_hbm.at[h], osem.at[1])
        c.start()
        outs.append(c)
        for l in reversed(range(LAYERS)):
            small += ag_copies[l]
        for c in small:
            c.wait_recv()
    else:
        c = pltpu.make_async_copy(sml, sm_hbm.at[0], osem.at[1])
        c.start()
        outs.append(c)
        for l in range(LAYERS):
            c = pltpu.make_async_copy(pg_out.at[l], pg_hbm.at[l], osem.at[2 + l])
            c.start()
            outs.append(c)
    for k in range(2 * LAYERS):
        halo_drain(k)
    for c in sends:
        c.wait_send()
    for c in outs:
        c.wait()


def finish(tg, pg, sm, tg_hbm, pg_hbm, tp_hbm, gn_hbm, tg_v, pg_in, sm_in, pg_v, tp_v, gn_v, sem):
    L, haps, _, Q = pg.shape
    Cq = sm.shape[2]
    loads = [
        pltpu.make_async_copy(a, b, sem.at[0, j]) for j, (a, b) in enumerate(((pg, pg_in), (tg, tg_v), (sm, sm_in)))]
    stores = [
        pltpu.make_async_copy(a, b, sem.at[1, j])
        for j, (a, b) in enumerate(((pg_v, pg_hbm), (tg_v, tg_hbm), (tp_v, tp_hbm), (gn_v, gn_hbm)))]
    for c in loads:
        c.start()
    loads[0].wait()
    for l in range(L):
        for q in range(haps):
            pg_v[l, :, q * Q : (q + 1) * Q] = pg_in[l, q].astype(F32)
    stores[0].start()
    loads[1].wait()
    stores[1].start()
    loads[2].wait()
    for q in range(haps):
        for j in range(3):
            tp_v[j, :, q * Cq : (q + 1) * Cq] = sm_in[q, j * L : (j + 1) * L, :]
        gn_v[:, q * Cq : (q + 1) * Cq] = sm_in[q, 3 * L :, :]
    stores[2].start()
    stores[3].start()
    for c in stores:
        c.wait()


def shards(n, haps, tokens, cotangent, gaps, conv_taps, norm_gains, projection):
    x = tokens[0]
    N, C = x.shape
    PR = projection.shape[2]
    inside = n > 2 and n % 2 == 0 and haps == 4 and C % (16 * n) == 0 and C % (128 * haps) == 0
    Cq, nz = C // haps, max(n // 2, 1)
    Q, rows = PR // haps, max(C // n, 1)
    L = LAYERS
    wide = haps if inside else 1

    def dma(*shape):
        return pltpu.SemaphoreType.DMA(shape)

    def opt(shape, dtype):
        return pltpu.VMEM(shape if inside else (16, 128), dtype)

    scratch = [
        pltpu.VMEM((N, C), BF16), pltpu.VMEM((N, C), BF16), pltpu.SMEM(gaps.shape, jnp.int32),
        pltpu.VMEM((3, L, C), F32), pltpu.VMEM((L, C), F32), dma(5),
        pltpu.VMEM((L, C, PR), BF16), dma(L),
        pltpu.VMEM((2 * L, 2, D, C), BF16), pltpu.VMEM((2 * L, 2, D, C), BF16), dma(2 * L, 2), dma(2 * L, 2),
        pltpu.VMEM((L, N, C), BF16), pltpu.VMEM((L, N, 1), F32), pltpu.VMEM((L, N + 2 * D, C), F32),
        pltpu.VMEM((L, N, C), F32), pltpu.VMEM((L, N, C), BF16), pltpu.VMEM((L, N, PR), F32),
        pltpu.VMEM((L, haps, N, Q), BF16), pltpu.VMEM((L, N + 2 * D, C), F32), pltpu.VMEM((N, C), F32),
        pltpu.VMEM((L, wide, C, N), BF16), dma(L, haps), dma(L, haps),
        opt((L, N * haps, Q), BF16), dma(L, haps, 3), dma(L, haps, 3),
        opt((L, n, rows, Q), BF16), opt((L, nz, rows, Q), BF16), dma(L, nz), dma(L, nz),
        opt((L, rows, Q), F32), opt((L, nz, rows, Q), BF16), opt((L, nz, rows, Q), BF16), dma(L, nz), dma(L, nz),
        opt((L, rows, Q), BF16), dma(L, haps), dma(L, haps),
        pltpu.VMEM((4 * L, C), F32), opt((haps, 4 * L, Cq), F32), dma(haps), dma(haps),
        opt((n, 4 * L, Cq), F32), dma(n), dma(n), opt((4 * L, Cq), F32), dma(haps), dma(haps),
    ]
    hbm = pl.BlockSpec(memory_space=pltpu.HBM)
    tg_shape = jax.ShapeDtypeStruct((N, C), BF16)
    outs = [
        tg_shape,
        jax.ShapeDtypeStruct((L, haps, rows, Q), BF16) if inside else jax.ShapeDtypeStruct((L, C, PR), F32),
        jax.ShapeDtypeStruct((haps, 4 * L, Cq) if inside else (1, 4 * L, C), F32)]
    scratch = [
        pltpu.VMEM((N, C), BF16), pltpu.VMEM((16, 128) if inside else (L, C, PR), F32), dma(2 + L)] + scratch
    params = dict(vmem_limit_bytes=60 * 1024 * 1024)
    tg, pg, sm = pl.pallas_call(
        functools.partial(kernel, n, haps, inside),
        out_shape=outs,
        in_specs=[hbm] * 6,
        out_specs=[hbm] * 3,
        scratch_shapes=scratch,
        compiler_params=pltpu.CompilerParams(collective_id=0, has_side_effects=True, **params),
    )(x, cotangent[0], gaps, jnp.transpose(conv_taps, (1, 0, 2)), norm_gains, projection)
    if inside:
        finals = [
            tg_shape, jax.ShapeDtypeStruct((L, rows, PR), F32),
            jax.ShapeDtypeStruct((3, L, C), F32), jax.ShapeDtypeStruct((L, C), F32)]
        tg, pg, taps, gains = pl.pallas_call(
            finish,
            out_shape=finals,
            in_specs=[hbm] * 3,
            out_specs=[hbm] * 4,
            scratch_shapes=[pltpu.VMEM(o.shape, o.dtype) for o in outs + finals[1:]] + [dma(2, 4)],
            compiler_params=pltpu.CompilerParams(**params),
        )(tg, pg, sm)
    else:
        pg = lax.psum(lax.psum_scatter(pg, "seq", scatter_dimension=1, tiled=True), "hap")
        sm = lax.psum(sm[0], ("seq", "hap"))
        taps, gains = sm[: 3 * L].reshape(3, L, C), sm[3 * L :]
    return tg[None], pg, jnp.transpose(taps, (1, 0, 2)), gains


def solution(mesh):
    return jax.shard_map(
        functools.partial(shards, mesh.shape["seq"], mesh.shape["hap"]),
        mesh=mesh,
        in_specs=(P("hap", "seq", None), P("hap", "seq", None), P("seq", None), P(), P(), P()),
        out_specs=(P("hap", "seq", None), P(None, "seq", None), P(), P()),
        check_vma=False,
    )
```

```python
import functools

import jax
import jax.numpy as jnp
from jax import lax
from jax.experimental import pallas as pl
from jax.experimental.pallas import tpu as pltpu
from jax.sharding import PartitionSpec as P

D = 32
LAYERS = 2
EPS = 1e-06
GELU_C = 0.7978845608028654
GELU_A = 0.044715
F32 = jnp.float32
BF16 = jnp.bfloat16
MESH = pl.DeviceIdType.MESH


def kernel(
    n, haps, inside,
    tok_hbm, cot_hbm, gaps_hbm, taps_hbm, gains_hbm, w_hbm,
    tg_hbm, pg_hbm, sm_hbm,
    tg_out, pg_out, osem, tok, cot, gaps, taps, gains, isem, w, wsem, edge_out, halo_in, hs, hr, xs, inv, npad, dgelu, hid, proj, dp, dpad, gcur,
    hT, hTs, hTr, dq_in, dqs, dqr, gbf, xr, xrs, xrr, own, zb, zr, zrs, zrr, ag, ags, agr, sml, smh, smhs, smhr, sms, smss, smsr, sma, smas, smar,
):
    me, h = lax.axis_index("seq"), lax.axis_index("hap")
    N, C = tok.shape
    PR = w.shape[2]
    Q, Cq = PR // haps, C // haps
    chunks = N // D
    outer, inner = (0, chunks - 1), tuple(range(1, chunks - 1))
    rows = C // n
    left, right = jnp.maximum(me - 1, 0), jnp.minimum(me + 1, n - 1)
    has_left, has_right = me > 0, me < n - 1
    sends = []

    loads = [pltpu.make_async_copy(w_hbm.at[l], w.at[l], wsem.at[l]) for l in range(LAYERS)]
    small_in = [
        pltpu.make_async_copy(a, b, isem.at[j])
        for j, (a, b) in enumerate(
            ((tok_hbm, tok), (gaps_hbm, gaps), (gains_hbm, gains), (taps_hbm, taps), (cot_hbm, cot)))
    ]
    for c in small_in[:4] + loads + small_in[4:]:
        c.start()

    barrier = pltpu.get_barrier_semaphore()
    if inside:
        for d in range(1, n):
            pl.semaphore_signal(barrier, inc=1, device_id={"seq": lax.rem(me + d, n)}, device_id_type=MESH)
        for d in range(1, haps):
            pl.semaphore_signal(barrier, inc=1, device_id={"hap": lax.rem(h + d, haps)}, device_id_type=MESH)
    else:
        @pl.when(has_left)
        def _():
            pl.semaphore_signal(barrier, inc=1, device_id={"seq": left}, device_id_type=MESH)

        @pl.when(has_right)
        def _():
            pl.semaphore_signal(barrier, inc=1, device_id={"seq": right}, device_id_type=MESH)

    offs = lax.broadcasted_iota(jnp.int32, (D, 1), 0)

    def valid_of(i):
        b = offs + i * D
        return jnp.where((b >= gaps[0, 0]) & (b < gaps[0, 1]), 0.0, 1.0).astype(F32)

    small_in[0].wait()
    small_in[1].wait()
    valid = [valid_of(i) for i in range(chunks)]

    def ds(i):
        return pl.ds(i * D, D)

    def halo(k):
        up = pltpu.make_async_remote_copy(
            src_ref=edge_out.at[k, 1], dst_ref=halo_in.at[k, 0], send_sem=hs.at[k, 1],
            recv_sem=hr.at[k, 0], device_id={"seq": right}, device_id_type=MESH)
        down = pltpu.make_async_remote_copy(
            src_ref=edge_out.at[k, 0], dst_ref=halo_in.at[k, 1], send_sem=hs.at[k, 0],
            recv_sem=hr.at[k, 1], device_id={"seq": left}, device_id_type=MESH)
        return up, down

    def halo_start(k):
        up, down = halo(k)

        @pl.when(has_right)
        def _():
            up.start()

        @pl.when(has_left)
        def _():
            down.start()

        @pl.when(jnp.logical_not(has_left))
        def _():
            halo_in[k, 0] = jnp.zeros((D, C), BF16)

        @pl.when(jnp.logical_not(has_right))
        def _():
            halo_in[k, 1] = jnp.zeros((D, C), BF16)

    def halo_wait(k):
        up, down = halo(k)

        @pl.when(has_left)
        def _():
            up.wait_recv()

        @pl.when(has_right)
        def _():
            down.wait_recv()

    def halo_drain(k):
        up, down = halo(k)

        @pl.when(has_right)
        def _():
            up.wait_send()

        @pl.when(has_left)
        def _():
            down.wait_send()

    core = h + 1 - 2 * lax.rem(h, 2)
    peers = (h, core, lax.rem(h + 2, haps), lax.rem(core + 2, haps))

    def to_hap(src_of, dst_of, ss, rr, which=(1, 2, 3), to=None):
        out = []
        for d in which:
            t = peers[d if to is None else to]
            c = pltpu.make_async_remote_copy(
                src_ref=src_of(t), dst_ref=dst_of(d), send_sem=ss(d), recv_sem=rr(d),
                device_id={"hap": t}, device_id_type=MESH)
            c.start()
            out.append(c)
        sends.extend(out)
        return out

    def to_seq(src_of, dst_of, ss, rr):
        out = []
        for d in range(1, n):
            t = lax.rem(me + d, n)
            c = pltpu.make_async_remote_copy(
                src_ref=src_of(t), dst_ref=dst_of(d), send_sem=ss(d), recv_sem=rr(d),
                device_id={"seq": t}, device_id_type=MESH)
            c.start()
            out.append(c)
        sends.extend(out)
        return out

    xs[0] = tok[...]
    edge_out[0, 0] = (tok[ds(0), :].astype(F32) * valid[0]).astype(BF16)
    edge_out[0, 1] = (tok[ds(chunks - 1), :].astype(F32) * valid[-1]).astype(BF16)
    if inside:
        pl.semaphore_wait(barrier, n - 1 + haps - 1)
    else:
        @pl.when(has_left)
        def _():
            pl.semaphore_wait(barrier, 1)

        @pl.when(has_right)
        def _():
            pl.semaphore_wait(barrier, 1)
    halo_start(0)
    small_in[2].wait()
    small_in[3].wait()

    def rms(x):
        return lax.rsqrt(jnp.mean(x * x, axis=-1, keepdims=True) + EPS)

    def forward_chunk(l, i):
        pre = (
            taps[0, l : l + 1, :] * npad[l, ds(i), :]
            + taps[1, l : l + 1, :] * npad[l, ds(i + 1), :]
            + taps[2, l : l + 1, :] * npad[l, ds(i + 2), :]
        )
        sq = pre * pre
        th = jnp.tanh(GELU_C * (pre + GELU_A * (sq * pre)))
        half = 0.5 * (1.0 + th)
        hidden = (pre * half).astype(BF16)
        hid[l, 0, ds(i), :] = hidden
        dgelu[l, ds(i), :] = half + 0.5 * pre * (1.0 - th * th) * (GELU_C * (1.0 + 3.0 * GELU_A * sq))

    hid_copies = [[[] for _ in range(4)] for _ in range(LAYERS)]

    def blocks_of(which):
        return [(0, D, N - 2 * D)] if which == inner else [(1, 0, D), (2, N - D, D)]

    def send_hidden(l, which):
        if not inside:
            return
        for j, start, size in blocks_of(which):
            near, far = to_hap(
                lambda t: hid.at[l, 0, pl.ds(start, size), :], lambda d: hid.at[l, d, pl.ds(start, size), :],
                lambda d: hTs.at[l, d, j], lambda d: hTr.at[l, d, j], (1, 2))
            hid_copies[l][1].append(near)
            hid_copies[l][2].append(far)

    def relay_hidden(l):
        if inside:
            for c in hid_copies[l][2]:
                c.wait_recv()
            hid_copies[l][2] = []
            hid_copies[l][3] = to_hap(
                lambda t: hid.at[l, 2], lambda d: hid.at[l, d],
                lambda d: hTs.at[l, d, 0], lambda d: hTr.at[l, d, 0], (3,), 1)

    def turn(l, which):
        for d in which:
            if d == 0 or inside:
                for c in hid_copies[l][d]:
                    c.wait_recv()
                hT[l, d] = jnp.transpose(hid[l, d].astype(F32)).astype(BF16)

    def norm_chunk(l, i):
        v = xs[l, ds(i), :].astype(F32)
        r = rms(v)
        inv[l, ds(i), :] = r
        npad[l, ds(i + 1), :] = v * r * gains[l : l + 1, :] * valid[i]

    def project(l, which):
        y = jnp.dot(
            jnp.concatenate([hid[l, 0, ds(i), :] for i in which], axis=0), w[l], preferred_element_type=F32)
        for j, i in enumerate(which):
            first = y[j * D : (j + 1) * D, 0:C]
            gate = 0.5 + 0.5 * jnp.tanh(0.5 * y[j * D : (j + 1) * D, C:PR])
            proj[l, ds(i), 0:C] = first
            proj[l, ds(i), C:PR] = gate
            if l + 1 < LAYERS:
                nxt = (xs[l, ds(i), :].astype(F32) + valid[i] * first * gate).astype(BF16)
                xs[l + 1, ds(i), :] = nxt
                if i in outer:
                    edge_out[l + 1, 0 if i == 0 else 1] = (nxt.astype(F32) * valid[i]).astype(BF16)

    def dproj(l, i):
        first = proj[l, ds(i), 0:C]
        gate = proj[l, ds(i), C:PR]
        grad = cot[ds(i), :].astype(F32) if l == LAYERS - 1 else gcur[ds(i), :]
        bg = valid[i] * grad * gate
        both = jnp.concatenate([bg, bg * first * (1.0 - gate)], axis=1).astype(BF16)
        for q in range(haps):
            dp[l, q, ds(i), :] = both[:, q * Q : (q + 1) * Q]

    def send_dproj(l, which):
        if not inside:
            return
        for j, start, size in blocks_of(which):
            dq_copies[l] += to_hap(
                lambda t: dp.at[l, t, pl.ds(start, size), :],
                lambda d: dq_in.at[l, pl.ds(d * N + start, size), :],
                lambda d: dqs.at[l, d, j], lambda d: dqr.at[l, d, j])

    def dconv(l, which):
        y = lax.dot_general(
            jnp.concatenate(
                [jnp.concatenate([dp[l, q, ds(i), :] for q in range(haps)], axis=1) for i in which], axis=0),
            w[l], (((1,), (1,)), ((), ())), preferred_element_type=F32)
        for j, i in enumerate(which):
            dpre = y[j * D : (j + 1) * D, :] * dgelu[l, ds(i), :]
            dpad[l, ds(i + 1), :] = dpre
            if i in outer:
                edge_out[2 * LAYERS - 1 - l, 0 if i == 0 else 1] = dpre.astype(BF16)

    def fold(v):
        return jnp.sum(v.reshape(D // 8, 8, C), axis=0)

    outs = []
    dq_copies, x_copies, z_copies, ag_copies = [[[] for _ in range(LAYERS)] for _ in range(4)]
    nz = n // 2
    z, x = me // 2, lax.rem(me, 2)
    order = [nz // 2] + [j for j in range(1, nz) if j != nz // 2] + [0]

    for l in range(LAYERS):
        last = l == LAYERS - 1
        for i in range(chunks):
            norm_chunk(l, i)
        for i in inner:
            forward_chunk(l, i)
        send_hidden(l, inner)
        loads[l].wait()
        project(l, inner)
        if last:
            small_in[4].wait()
            for i in inner:
                dproj(l, i)
            send_dproj(l, inner)
            dconv(l, inner)
        halo_wait(l)
        for side, at in ((0, 0), (1, chunks + 1)):
            v = halo_in[l, side].astype(F32)
            npad[l, ds(at), :] = v * rms(v) * gains[l : l + 1, :]
        for i in outer:
            forward_chunk(l, i)
        project(l, outer)
        if last:
            for i in outer:
                dproj(l, i)
            dconv(l, outer)
        halo_start(l + 1)
        send_hidden(l, outer)
        if last:
            send_dproj(l, outer)

    def gram(l):
        if not inside:
            pg_out[l] = jnp.dot(
                hT[l, 0], jnp.concatenate([dp[l, q] for q in range(haps)], axis=1), preferred_element_type=F32)
            return
        dq_in[l, 0:N, :] = dp[l, h]
        for c in dq_copies[l]:
            c.wait_recv()
        g = jnp.dot(
            jnp.concatenate([hT[l, d] for d in range(haps)], axis=1), dq_in[l], preferred_element_type=F32)
        gbf[l] = g.astype(BF16).reshape(n, rows, Q)
        for j in order:
            c = pltpu.make_async_remote_copy(
                src_ref=gbf.at[l, 2 * lax.rem(z + j, nz) + 1 - x], dst_ref=xr.at[l, j],
                send_sem=xrs.at[l, j], recv_sem=xrr.at[l, j],
                device_id={"seq": 2 * z + 1 - x}, device_id_type=MESH)
            c.start()
            x_copies[l].append(c)
        sends.extend(x_copies[l])

    def forward(l):
        for j, c in zip(order, x_copies[l]):
            t = 2 * lax.rem(z + j, nz) + x
            c.wait_recv()
            total = gbf[l, t].astype(F32) + xr[l, j].astype(F32)
            if j == 0:
                own[l] = total
                continue
            zb[l, j] = total.astype(BF16)
            c = pltpu.make_async_remote_copy(
                src_ref=zb.at[l, j], dst_ref=zr.at[l, j], send_sem=zrs.at[l, j], recv_sem=zrr.at[l, j],
                device_id={"seq": t}, device_id_type=MESH)
            c.start()
            z_copies[l].append((j, c))
            sends.append(c)

    def reduced(l):
        total = own[l]
        for j, c in z_copies[l]:
            c.wait_recv()
            total = total + zr[l, j].astype(F32)
        ag[l] = total.astype(BF16)
        ag_copies[l] = to_hap(
            lambda t: ag.at[l], lambda d: pg_hbm.at[l, h], lambda d: ags.at[l, d], lambda d: agr.at[l, d])
        c = pltpu.make_async_copy(ag.at[l], pg_hbm.at[l, h], osem.at[2 + l])
        c.start()
        outs.append(c)

    for l in reversed(range(LAYERS)):
        k = 2 * LAYERS - 1 - l
        last = l == LAYERS - 1
        g_sum = jnp.zeros((8, C), F32)

        def back_chunk(i, g_sum):
            dn = (
                taps[0, l : l + 1, :] * dpad[l, ds(i + 2), :]
                + taps[1, l : l + 1, :] * dpad[l, ds(i + 1), :]
                + taps[2, l : l + 1, :] * dpad[l, ds(i), :]
            )
            dq = dn * valid[i]
            v = xs[l, ds(i), :].astype(F32)
            r = inv[l, ds(i), :]
            vr = v * r
            g_sum = g_sum + fold(dq * vr)
            dt = dq * gains[l : l + 1, :]
            grad = cot[ds(i), :].astype(F32) if last else gcur[ds(i), :]
            new = grad + r * dt - vr * (r * r * jnp.mean(dt * v, axis=-1, keepdims=True))
            if l == 0:
                tg_out[ds(i), :] = new.astype(BF16)
            else:
                gcur[ds(i), :] = new
                dproj(l - 1, i)
            return g_sum

        for i in inner:
            g_sum = back_chunk(i, g_sum)
        if l > 0:
            send_dproj(l - 1, inner)
            relay_hidden(l - 1)
            dconv(l - 1, inner)
            turn(l - 1, (0, 1, 2))
            if last:
                turn(l, (0,))
        t_sum = [jnp.zeros((8, C), F32) for _ in range(3)]
        for i in range(chunks):
            dpre = dpad[l, ds(i + 1), :]
            for j in range(3):
                t_sum[j] = t_sum[j] + fold(dpre * npad[l, ds(i + j), :])
        for j in range(3):
            sml[LAYERS * j + l : LAYERS * j + l + 1, :] = jnp.sum(t_sum[j], axis=0, keepdims=True)
        if l == 0:
            turn(0, (3,))
            gram(0)
            if inside:
                for m in range(1, LAYERS):
                    forward(m)
        halo_wait(k)
        dpad[l, ds(0), :] = halo_in[k, 0].astype(F32)
        dpad[l, ds(chunks + 1), :] = halo_in[k, 1].astype(F32)
        for i in outer:
            g_sum = back_chunk(i, g_sum)
        if l > 0:
            send_dproj(l - 1, outer)
            dconv(l - 1, outer)
            halo_start(k + 1)
            if last:
                relay_hidden(l)
                turn(l, (1, 2))
            turn(l, (3,))
            gram(l)
        sml[3 * LAYERS + l : 3 * LAYERS + l + 1, :] = jnp.sum(g_sum, axis=0, keepdims=True)

    c = pltpu.make_async_copy(tg_out, tg_hbm, osem.at[0])
    c.start()
    outs.append(c)
    if inside:
        def quarter(t):
            return pl.ds(pl.multiple_of(t * Cq, Cq), Cq)

        smh[h] = sml[:, quarter(h)]
        small = to_hap(
            lambda t: sml.at[:, quarter(t)], lambda d: smh.at[h], lambda d: smhs.at[d], lambda d: smhr.at[d])
        forward(0)
        for c in small:
            c.wait_recv()
        total = smh[0]
        for q in range(1, haps):
            total = total + smh[q]
        sms[me] = total
        small = to_seq(lambda t: sms.at[me], lambda d: sms.at[me], lambda d: smss.at[d], lambda d: smsr.at[d])
        for l in range(1, LAYERS):
            reduced(l)
        reduced(0)
        for c in small:
            c.wait_recv()
        total = sms[0]
        for q in range(1, n):
            total = total + sms[q]
        sma[...] = total
        small = to_hap(lambda t: sma, lambda d: sm_hbm.at[h], lambda d: smas.at[d], lambda d: smar.at[d])
        c = pltpu.make_async_copy(sma, sm_hbm.at[h], osem.at[1])
        c.start()
        outs.append(c)
        for l in reversed(range(LAYERS)):
            small += ag_copies[l]
        for c in small:
            c.wait_recv()
    else:
        c = pltpu.make_async_copy(sml, sm_hbm.at[0], osem.at[1])
        c.start()
        outs.append(c)
        for l in range(LAYERS):
            c = pltpu.make_async_copy(pg_out.at[l], pg_hbm.at[l], osem.at[2 + l])
            c.start()
            outs.append(c)
    for k in range(2 * LAYERS):
        halo_drain(k)
    for c in sends:
        c.wait_send()
    for c in outs:
        c.wait()


def finish(tg, pg, sm, tg_hbm, pg_hbm, tp_hbm, gn_hbm, tg_v, pg_in, sm_in, pg_v, tp_v, gn_v, sem):
    L, haps, _, Q = pg.shape
    Cq = sm.shape[2]
    loads = [
        pltpu.make_async_copy(a, b, sem.at[0, j]) for j, (a, b) in enumerate(((pg, pg_in), (tg, tg_v), (sm, sm_in)))]
    stores = [
        pltpu.make_async_copy(a, b, sem.at[1, j])
        for j, (a, b) in enumerate(((pg_v, pg_hbm), (tg_v, tg_hbm), (tp_v, tp_hbm), (gn_v, gn_hbm)))]
    for c in loads:
        c.start()
    loads[0].wait()
    for l in range(L):
        for q in range(haps):
            pg_v[l, :, q * Q : (q + 1) * Q] = pg_in[l, q].astype(F32)
    stores[0].start()
    loads[1].wait()
    stores[1].start()
    loads[2].wait()
    for q in range(haps):
        for j in range(3):
            tp_v[j, :, q * Cq : (q + 1) * Cq] = sm_in[q, j * L : (j + 1) * L, :]
        gn_v[:, q * Cq : (q + 1) * Cq] = sm_in[q, 3 * L :, :]
    stores[2].start()
    stores[3].start()
    for c in stores:
        c.wait()


def shards(n, haps, tokens, cotangent, gaps, conv_taps, norm_gains, projection):
    x = tokens[0]
    N, C = x.shape
    PR = projection.shape[2]
    inside = n > 2 and n % 2 == 0 and haps == 4 and C % (16 * n) == 0 and C % (128 * haps) == 0
    Cq, nz = C // haps, max(n // 2, 1)
    Q, rows = PR // haps, max(C // n, 1)
    L = LAYERS
    wide = haps if inside else 1

    def dma(*shape):
        return pltpu.SemaphoreType.DMA(shape)

    def opt(shape, dtype):
        return pltpu.VMEM(shape if inside else (16, 128), dtype)

    scratch = [
        pltpu.VMEM((N, C), BF16), pltpu.VMEM((N, C), BF16), pltpu.SMEM(gaps.shape, jnp.int32),
        pltpu.VMEM((3, L, C), F32), pltpu.VMEM((L, C), F32), dma(5),
        pltpu.VMEM((L, C, PR), BF16), dma(L),
        pltpu.VMEM((2 * L, 2, D, C), BF16), pltpu.VMEM((2 * L, 2, D, C), BF16), dma(2 * L, 2), dma(2 * L, 2),
        pltpu.VMEM((L, N, C), BF16), pltpu.VMEM((L, N, 1), F32), pltpu.VMEM((L, N + 2 * D, C), F32),
        pltpu.VMEM((L, N, C), F32), pltpu.VMEM((L, wide, N, C), BF16), pltpu.VMEM((L, N, PR), F32),
        pltpu.VMEM((L, haps, N, Q), BF16), pltpu.VMEM((L, N + 2 * D, C), F32), pltpu.VMEM((N, C), F32),
        pltpu.VMEM((L, wide, C, N), BF16), dma(L, haps, 3), dma(L, haps, 3),
        opt((L, N * haps, Q), BF16), dma(L, haps, 3), dma(L, haps, 3),
        opt((L, n, rows, Q), BF16), opt((L, nz, rows, Q), BF16), dma(L, nz), dma(L, nz),
        opt((L, rows, Q), F32), opt((L, nz, rows, Q), BF16), opt((L, nz, rows, Q), BF16), dma(L, nz), dma(L, nz),
        opt((L, rows, Q), BF16), dma(L, haps), dma(L, haps),
        pltpu.VMEM((4 * L, C), F32), opt((haps, 4 * L, Cq), F32), dma(haps), dma(haps),
        opt((n, 4 * L, Cq), F32), dma(n), dma(n), opt((4 * L, Cq), F32), dma(haps), dma(haps),
    ]
    hbm = pl.BlockSpec(memory_space=pltpu.HBM)
    tg_shape = jax.ShapeDtypeStruct((N, C), BF16)
    outs = [
        tg_shape,
        jax.ShapeDtypeStruct((L, haps, rows, Q), BF16) if inside else jax.ShapeDtypeStruct((L, C, PR), F32),
        jax.ShapeDtypeStruct((haps, 4 * L, Cq) if inside else (1, 4 * L, C), F32)]
    scratch = [
        pltpu.VMEM((N, C), BF16), pltpu.VMEM((16, 128) if inside else (L, C, PR), F32), dma(2 + L)] + scratch
    params = dict(vmem_limit_bytes=60 * 1024 * 1024)
    tg, pg, sm = pl.pallas_call(
        functools.partial(kernel, n, haps, inside),
        out_shape=outs,
        in_specs=[hbm] * 6,
        out_specs=[hbm] * 3,
        scratch_shapes=scratch,
        compiler_params=pltpu.CompilerParams(collective_id=0, has_side_effects=True, **params),
    )(x, cotangent[0], gaps, jnp.transpose(conv_taps, (1, 0, 2)), norm_gains, projection)
    if inside:
        finals = [
            tg_shape, jax.ShapeDtypeStruct((L, rows, PR), F32),
            jax.ShapeDtypeStruct((3, L, C), F32), jax.ShapeDtypeStruct((L, C), F32)]
        tg, pg, taps, gains = pl.pallas_call(
            finish,
            out_shape=finals,
            in_specs=[hbm] * 3,
            out_specs=[hbm] * 4,
            scratch_shapes=[pltpu.VMEM(o.shape, o.dtype) for o in outs + finals[1:]] + [dma(2, 4)],
            compiler_params=pltpu.CompilerParams(**params),
        )(tg, pg, sm)
    else:
        pg = lax.psum(lax.psum_scatter(pg, "seq", scatter_dimension=1, tiled=True), "hap")
        sm = lax.psum(sm[0], ("seq", "hap"))
        taps, gains = sm[: 3 * L].reshape(3, L, C), sm[3 * L :]
    return tg[None], pg, jnp.transpose(taps, (1, 0, 2)), gains


def solution(mesh):
    return jax.shard_map(
        functools.partial(shards, mesh.shape["seq"], mesh.shape["hap"]),
        mesh=mesh,
        in_specs=(P("hap", "seq", None), P("hap", "seq", None), P("seq", None), P(), P(), P()),
        out_specs=(P("hap", "seq", None), P(None, "seq", None), P(), P()),
        check_vma=False,
    )
```

```python
import functools

import jax
import jax.numpy as jnp
from jax import lax
from jax.experimental import pallas as pl
from jax.experimental.pallas import tpu as pltpu
from jax.sharding import PartitionSpec as P

D = 32
LAYERS = 2
EPS = 1e-06
GELU_C = 0.7978845608028654
GELU_A = 0.044715
F32 = jnp.float32
BF16 = jnp.bfloat16
MESH = pl.DeviceIdType.MESH


def kernel(
    n, haps, inside,
    tok_hbm, cot_hbm, gaps_hbm, taps_hbm, gains_hbm, w_hbm,
    tg_hbm, pg_hbm, sm_hbm,
    tg_out, pg_out, osem, tok, cot, gaps, taps, gains, isem, w, wsem, edge_out, halo_in, hs, hr, xs, inv, npad, dgelu, hid, proj, dp, dpad, gcur,
    hT, hTs, hTr, dq_in, dqs, dqr, gbf, xr, xrs, xrr, own, zb, zr, zrs, zrr, ag, ags, agr, sml, smh, smhs, smhr, sms, smss, smsr, sma, smas, smar,
):
    me, h = lax.axis_index("seq"), lax.axis_index("hap")
    N, C = tok.shape
    PR = w.shape[2]
    Q, Cq = PR // haps, C // haps
    chunks = N // D
    outer, inner = (0, chunks - 1), tuple(range(1, chunks - 1))
    rows = C // n
    left, right = jnp.maximum(me - 1, 0), jnp.minimum(me + 1, n - 1)
    has_left, has_right = me > 0, me < n - 1
    sends = []

    loads = [pltpu.make_async_copy(w_hbm.at[l], w.at[l], wsem.at[l]) for l in range(LAYERS)]
    small_in = [
        pltpu.make_async_copy(a, b, isem.at[j])
        for j, (a, b) in enumerate(
            ((tok_hbm, tok), (gaps_hbm, gaps), (gains_hbm, gains), (taps_hbm, taps), (cot_hbm, cot)))
    ]
    for c in small_in[:4] + loads + small_in[4:]:
        c.start()

    barrier = pltpu.get_barrier_semaphore()
    if inside:
        for d in range(1, n):
            pl.semaphore_signal(barrier, inc=1, device_id={"seq": lax.rem(me + d, n)}, device_id_type=MESH)
        for d in range(1, haps):
            pl.semaphore_signal(barrier, inc=1, device_id={"hap": lax.rem(h + d, haps)}, device_id_type=MESH)
    else:
        @pl.when(has_left)
        def _():
            pl.semaphore_signal(barrier, inc=1, device_id={"seq": left}, device_id_type=MESH)

        @pl.when(has_right)
        def _():
            pl.semaphore_signal(barrier, inc=1, device_id={"seq": right}, device_id_type=MESH)

    offs = lax.broadcasted_iota(jnp.int32, (D, 1), 0)

    def valid_of(i):
        b = offs + i * D
        return jnp.where((b >= gaps[0, 0]) & (b < gaps[0, 1]), 0.0, 1.0).astype(F32)

    small_in[0].wait()
    small_in[1].wait()
    valid = [valid_of(i) for i in range(chunks)]

    def ds(i):
        return pl.ds(i * D, D)

    def halo(k):
        up = pltpu.make_async_remote_copy(
            src_ref=edge_out.at[k, 1], dst_ref=halo_in.at[k, 0], send_sem=hs.at[k, 1],
            recv_sem=hr.at[k, 0], device_id={"seq": right}, device_id_type=MESH)
        down = pltpu.make_async_remote_copy(
            src_ref=edge_out.at[k, 0], dst_ref=halo_in.at[k, 1], send_sem=hs.at[k, 0],
            recv_sem=hr.at[k, 1], device_id={"seq": left}, device_id_type=MESH)
        return up, down

    def halo_start(k):
        up, down = halo(k)

        @pl.when(has_right)
        def _():
            up.start()

        @pl.when(has_left)
        def _():
            down.start()

        @pl.when(jnp.logical_not(has_left))
        def _():
            halo_in[k, 0] = jnp.zeros((D, C), BF16)

        @pl.when(jnp.logical_not(has_right))
        def _():
            halo_in[k, 1] = jnp.zeros((D, C), BF16)

    def halo_wait(k):
        up, down = halo(k)

        @pl.when(has_left)
        def _():
            up.wait_recv()

        @pl.when(has_right)
        def _():
            down.wait_recv()

    def halo_drain(k):
        up, down = halo(k)

        @pl.when(has_right)
        def _():
            up.wait_send()

        @pl.when(has_left)
        def _():
            down.wait_send()

    core = h + 1 - 2 * lax.rem(h, 2)
    peers = (h, core, lax.rem(h + 2, haps), lax.rem(core + 2, haps))

    def to_hap(src_of, dst_of, ss, rr, which=(1, 2, 3), to=None):
        out = []
        for d in which:
            t = peers[d if to is None else to]
            c = pltpu.make_async_remote_copy(
                src_ref=src_of(t), dst_ref=dst_of(d), send_sem=ss(d), recv_sem=rr(d),
                device_id={"hap": t}, device_id_type=MESH)
            c.start()
            out.append(c)
        sends.extend(out)
        return out

    def to_seq(src_of, dst_of, ss, rr):
        out = []
        for d in range(1, n):
            t = lax.rem(me + d, n)
            c = pltpu.make_async_remote_copy(
                src_ref=src_of(t), dst_ref=dst_of(d), send_sem=ss(d), recv_sem=rr(d),
                device_id={"seq": t}, device_id_type=MESH)
            c.start()
            out.append(c)
        sends.extend(out)
        return out

    xs[0] = tok[...]
    edge_out[0, 0] = (tok[ds(0), :].astype(F32) * valid[0]).astype(BF16)
    edge_out[0, 1] = (tok[ds(chunks - 1), :].astype(F32) * valid[-1]).astype(BF16)
    if inside:
        pl.semaphore_wait(barrier, n - 1 + haps - 1)
    else:
        @pl.when(has_left)
        def _():
            pl.semaphore_wait(barrier, 1)

        @pl.when(has_right)
        def _():
            pl.semaphore_wait(barrier, 1)
    halo_start(0)
    small_in[2].wait()
    small_in[3].wait()

    def rms(x):
        return lax.rsqrt(jnp.mean(x * x, axis=-1, keepdims=True) + EPS)

    def forward_chunk(l, i):
        pre = (
            taps[0, l : l + 1, :] * npad[l, ds(i), :]
            + taps[1, l : l + 1, :] * npad[l, ds(i + 1), :]
            + taps[2, l : l + 1, :] * npad[l, ds(i + 2), :]
        )
        sq = pre * pre
        th = jnp.tanh(GELU_C * (pre + GELU_A * (sq * pre)))
        half = 0.5 * (1.0 + th)
        hidden = (pre * half).astype(BF16)
        hid[l, 0, ds(i), :] = hidden
        dgelu[l, ds(i), :] = half + 0.5 * pre * (1.0 - th * th) * (GELU_C * (1.0 + 3.0 * GELU_A * sq))

    hid_copies = [[[] for _ in range(4)] for _ in range(LAYERS)]

    def blocks_of(which):
        return [(0, D, N - 2 * D)] if which == inner else [(1, 0, D), (2, N - D, D)]

    def send_hidden(l, which):
        if not inside:
            return
        for j, start, size in blocks_of(which):
            near, far = to_hap(
                lambda t: hid.at[l, 0, pl.ds(start, size), :], lambda d: hid.at[l, d, pl.ds(start, size), :],
                lambda d: hTs.at[l, d, j], lambda d: hTr.at[l, d, j], (1, 2))
            hid_copies[l][1].append(near)
            hid_copies[l][2].append(far)

    def relay_hidden(l):
        if inside:
            for c in hid_copies[l][2]:
                c.wait_recv()
            hid_copies[l][2] = []
            hid_copies[l][3] = to_hap(
                lambda t: hid.at[l, 2], lambda d: hid.at[l, d],
                lambda d: hTs.at[l, d, 0], lambda d: hTr.at[l, d, 0], (3,), 1)

    def turn(l, which):
        for d in which:
            if d == 0 or inside:
                for c in hid_copies[l][d]:
                    c.wait_recv()
                hT[l, d] = jnp.transpose(hid[l, d].astype(F32)).astype(BF16)

    def norm_chunk(l, i):
        v = xs[l, ds(i), :].astype(F32)
        r = rms(v)
        inv[l, ds(i), :] = r
        npad[l, ds(i + 1), :] = v * r * gains[l : l + 1, :] * valid[i]

    def project(l, which):
        y = jnp.dot(
            jnp.concatenate([hid[l, 0, ds(i), :] for i in which], axis=0), w[l], preferred_element_type=F32)
        for j, i in enumerate(which):
            first = y[j * D : (j + 1) * D, 0:C]
            gate = 0.5 + 0.5 * jnp.tanh(0.5 * y[j * D : (j + 1) * D, C:PR])
            proj[l, ds(i), 0:C] = first
            proj[l, ds(i), C:PR] = gate
            if l + 1 < LAYERS:
                nxt = (xs[l, ds(i), :].astype(F32) + valid[i] * first * gate).astype(BF16)
                xs[l + 1, ds(i), :] = nxt
                if i in outer:
                    edge_out[l + 1, 0 if i == 0 else 1] = (nxt.astype(F32) * valid[i]).astype(BF16)

    def dproj(l, i):
        first = proj[l, ds(i), 0:C]
        gate = proj[l, ds(i), C:PR]
        grad = cot[ds(i), :].astype(F32) if l == LAYERS - 1 else gcur[ds(i), :]
        bg = valid[i] * grad * gate
        both = jnp.concatenate([bg, bg * first * (1.0 - gate)], axis=1).astype(BF16)
        for q in range(haps):
            dp[l, q, ds(i), :] = both[:, q * Q : (q + 1) * Q]

    def send_dproj(l, which):
        if not inside:
            return
        for j, start, size in blocks_of(which):
            dq_copies[l] += to_hap(
                lambda t: dp.at[l, t, pl.ds(start, size), :],
                lambda d: dq_in.at[l, pl.ds(d * N + start, size), :],
                lambda d: dqs.at[l, d, j], lambda d: dqr.at[l, d, j])

    def dconv(l, which):
        y = lax.dot_general(
            jnp.concatenate(
                [jnp.concatenate([dp[l, q, ds(i), :] for q in range(haps)], axis=1) for i in which], axis=0),
            w[l], (((1,), (1,)), ((), ())), preferred_element_type=F32)
        for j, i in enumerate(which):
            dpre = y[j * D : (j + 1) * D, :] * dgelu[l, ds(i), :]
            dpad[l, ds(i + 1), :] = dpre
            if i in outer:
                edge_out[2 * LAYERS - 1 - l, 0 if i == 0 else 1] = dpre.astype(BF16)

    def fold(v):
        return jnp.sum(v.reshape(D // 8, 8, C), axis=0)

    outs = []
    dq_copies, x_copies, z_copies, ag_copies = [[[] for _ in range(LAYERS)] for _ in range(4)]
    nz = n // 2
    z, x = me // 2, lax.rem(me, 2)
    order = [nz // 2] + [j for j in range(1, nz) if j != nz // 2] + [0]

    for l in range(LAYERS):
        last = l == LAYERS - 1
        for i in range(chunks):
            norm_chunk(l, i)
        for i in inner:
            forward_chunk(l, i)
        send_hidden(l, inner)
        loads[l].wait()
        project(l, inner)
        if last:
            small_in[4].wait()
            for i in inner:
                dproj(l, i)
            send_dproj(l, inner)
            dconv(l, inner)
        halo_wait(l)
        for side, at in ((0, 0), (1, chunks + 1)):
            v = halo_in[l, side].astype(F32)
            npad[l, ds(at), :] = v * rms(v) * gains[l : l + 1, :]
        for i in outer:
            forward_chunk(l, i)
        project(l, outer)
        if last:
            for i in outer:
                dproj(l, i)
            dconv(l, outer)
        halo_start(l + 1)
        send_hidden(l, outer)
        if last:
            send_dproj(l, outer)

    def gram(l):
        if not inside:
            pg_out[l] = jnp.dot(
                hT[l, 0], jnp.concatenate([dp[l, q] for q in range(haps)], axis=1), preferred_element_type=F32)
            return
        dq_in[l, 0:N, :] = dp[l, h]
        for c in dq_copies[l]:
            c.wait_recv()
        for j in order:
            t = lax.rem(z + j, nz)
            cut = pl.ds(pl.multiple_of(t * 2 * rows, 2 * rows), 2 * rows)
            g = jnp.dot(
                jnp.concatenate([hT[l, d, cut, :] for d in range(haps)], axis=1), dq_in[l],
                preferred_element_type=F32)
            gbf[l, pl.ds(2 * t, 2)] = g.astype(BF16).reshape(2, rows, Q)
            c = pltpu.make_async_remote_copy(
                src_ref=gbf.at[l, 2 * t + 1 - x], dst_ref=xr.at[l, j],
                send_sem=xrs.at[l, j], recv_sem=xrr.at[l, j],
                device_id={"seq": 2 * z + 1 - x}, device_id_type=MESH)
            c.start()
            x_copies[l].append(c)
        sends.extend(x_copies[l])

    def forward(l):
        for j, c in zip(order, x_copies[l]):
            t = 2 * lax.rem(z + j, nz) + x
            c.wait_recv()
            total = gbf[l, t].astype(F32) + xr[l, j].astype(F32)
            if j == 0:
                own[l] = total
                continue
            zb[l, j] = total.astype(BF16)
            c = pltpu.make_async_remote_copy(
                src_ref=zb.at[l, j], dst_ref=zr.at[l, j], send_sem=zrs.at[l, j], recv_sem=zrr.at[l, j],
                device_id={"seq": t}, device_id_type=MESH)
            c.start()
            z_copies[l].append((j, c))
            sends.append(c)

    def reduced(l):
        total = own[l]
        for j, c in z_copies[l]:
            c.wait_recv()
            total = total + zr[l, j].astype(F32)
        ag[l] = total.astype(BF16)
        ag_copies[l] = to_hap(
            lambda t: ag.at[l], lambda d: pg_hbm.at[l, h], lambda d: ags.at[l, d], lambda d: agr.at[l, d])
        c = pltpu.make_async_copy(ag.at[l], pg_hbm.at[l, h], osem.at[2 + l])
        c.start()
        outs.append(c)

    def tap_sums(l):
        t_sum = [jnp.zeros((8, C), F32) for _ in range(3)]
        for i in range(chunks):
            dpre = dpad[l, ds(i + 1), :]
            for j in range(3):
                t_sum[j] = t_sum[j] + fold(dpre * npad[l, ds(i + j), :])
        for j in range(3):
            sml[LAYERS * j + l : LAYERS * j + l + 1, :] = jnp.sum(t_sum[j], axis=0, keepdims=True)

    for l in reversed(range(LAYERS)):
        k = 2 * LAYERS - 1 - l
        last = l == LAYERS - 1
        g_sum = jnp.zeros((8, C), F32)

        def back_chunk(i, g_sum):
            dn = (
                taps[0, l : l + 1, :] * dpad[l, ds(i + 2), :]
                + taps[1, l : l + 1, :] * dpad[l, ds(i + 1), :]
                + taps[2, l : l + 1, :] * dpad[l, ds(i), :]
            )
            dq = dn * valid[i]
            v = xs[l, ds(i), :].astype(F32)
            r = inv[l, ds(i), :]
            vr = v * r
            g_sum = g_sum + fold(dq * vr)
            dt = dq * gains[l : l + 1, :]
            grad = cot[ds(i), :].astype(F32) if last else gcur[ds(i), :]
            new = grad + r * dt - vr * (r * r * jnp.mean(dt * v, axis=-1, keepdims=True))
            if l == 0:
                tg_out[ds(i), :] = new.astype(BF16)
            else:
                gcur[ds(i), :] = new
                dproj(l - 1, i)
            return g_sum

        if l == 0:
            turn(0, (3,))
            gram(0)
            for m in range(LAYERS):
                tap_sums(m)
        for i in inner:
            g_sum = back_chunk(i, g_sum)
        if l > 0:
            send_dproj(l - 1, inner)
            relay_hidden(l - 1)
            dconv(l - 1, inner)
            turn(l - 1, (0, 1, 2))
            if last:
                turn(l, (0,))
        if l == 0:
            if inside:
                for m in range(1, LAYERS):
                    forward(m)
        halo_wait(k)
        dpad[l, ds(0), :] = halo_in[k, 0].astype(F32)
        dpad[l, ds(chunks + 1), :] = halo_in[k, 1].astype(F32)
        for i in outer:
            g_sum = back_chunk(i, g_sum)
        if l > 0:
            send_dproj(l - 1, outer)
            dconv(l - 1, outer)
            halo_start(k + 1)
            if last:
                relay_hidden(l)
                turn(l, (1, 2))
            turn(l, (3,))
            gram(l)
        sml[3 * LAYERS + l : 3 * LAYERS + l + 1, :] = jnp.sum(g_sum, axis=0, keepdims=True)

    c = pltpu.make_async_copy(tg_out, tg_hbm, osem.at[0])
    c.start()
    outs.append(c)
    if inside:
        def quarter(t):
            return pl.ds(pl.multiple_of(t * Cq, Cq), Cq)

        smh[h] = sml[:, quarter(h)]
        small = to_hap(
            lambda t: sml.at[:, quarter(t)], lambda d: smh.at[h], lambda d: smhs.at[d], lambda d: smhr.at[d])
        forward(0)
        for c in small:
            c.wait_recv()
        total = smh[0]
        for q in range(1, haps):
            total = total + smh[q]
        sms[me] = total
        small = to_seq(lambda t: sms.at[me], lambda d: sms.at[me], lambda d: smss.at[d], lambda d: smsr.at[d])
        for l in range(1, LAYERS):
            reduced(l)
        reduced(0)
        for c in small:
            c.wait_recv()
        total = sms[0]
        for q in range(1, n):
            total = total + sms[q]
        sma[...] = total
        small = to_hap(lambda t: sma, lambda d: sm_hbm.at[h], lambda d: smas.at[d], lambda d: smar.at[d])
        c = pltpu.make_async_copy(sma, sm_hbm.at[h], osem.at[1])
        c.start()
        outs.append(c)
        for l in reversed(range(LAYERS)):
            small += ag_copies[l]
        for c in small:
            c.wait_recv()
    else:
        c = pltpu.make_async_copy(sml, sm_hbm.at[0], osem.at[1])
        c.start()
        outs.append(c)
        for l in range(LAYERS):
            c = pltpu.make_async_copy(pg_out.at[l], pg_hbm.at[l], osem.at[2 + l])
            c.start()
            outs.append(c)
    for k in range(2 * LAYERS):
        halo_drain(k)
    for c in sends:
        c.wait_send()
    for c in outs:
        c.wait()


def finish(tg, pg, sm, tg_hbm, pg_hbm, tp_hbm, gn_hbm, tg_v, pg_in, sm_in, pg_v, tp_v, gn_v, sem):
    L, haps, _, Q = pg.shape
    Cq = sm.shape[2]
    loads = [
        pltpu.make_async_copy(a, b, sem.at[0, j]) for j, (a, b) in enumerate(((pg, pg_in), (tg, tg_v), (sm, sm_in)))]
    stores = [
        pltpu.make_async_copy(a, b, sem.at[1, j])
        for j, (a, b) in enumerate(((pg_v, pg_hbm), (tg_v, tg_hbm), (tp_v, tp_hbm), (gn_v, gn_hbm)))]
    for c in loads:
        c.start()
    loads[0].wait()
    for l in range(L):
        for q in range(haps):
            pg_v[l, :, q * Q : (q + 1) * Q] = pg_in[l, q].astype(F32)
    stores[0].start()
    loads[1].wait()
    stores[1].start()
    loads[2].wait()
    for q in range(haps):
        for j in range(3):
            tp_v[j, :, q * Cq : (q + 1) * Cq] = sm_in[q, j * L : (j + 1) * L, :]
        gn_v[:, q * Cq : (q + 1) * Cq] = sm_in[q, 3 * L :, :]
    stores[2].start()
    stores[3].start()
    for c in stores:
        c.wait()


def shards(n, haps, tokens, cotangent, gaps, conv_taps, norm_gains, projection):
    x = tokens[0]
    N, C = x.shape
    PR = projection.shape[2]
    inside = n > 2 and n % 2 == 0 and haps == 4 and C % (16 * n) == 0 and C % (128 * haps) == 0
    Cq, nz = C // haps, max(n // 2, 1)
    Q, rows = PR // haps, max(C // n, 1)
    L = LAYERS
    wide = haps if inside else 1

    def dma(*shape):
        return pltpu.SemaphoreType.DMA(shape)

    def opt(shape, dtype):
        return pltpu.VMEM(shape if inside else (16, 128), dtype)

    scratch = [
        pltpu.VMEM((N, C), BF16), pltpu.VMEM((N, C), BF16), pltpu.SMEM(gaps.shape, jnp.int32),
        pltpu.VMEM((3, L, C), F32), pltpu.VMEM((L, C), F32), dma(5),
        pltpu.VMEM((L, C, PR), BF16), dma(L),
        pltpu.VMEM((2 * L, 2, D, C), BF16), pltpu.VMEM((2 * L, 2, D, C), BF16), dma(2 * L, 2), dma(2 * L, 2),
        pltpu.VMEM((L, N, C), BF16), pltpu.VMEM((L, N, 1), F32), pltpu.VMEM((L, N + 2 * D, C), F32),
        pltpu.VMEM((L, N, C), F32), pltpu.VMEM((L, wide, N, C), BF16), pltpu.VMEM((L, N, PR), F32),
        pltpu.VMEM((L, haps, N, Q), BF16), pltpu.VMEM((L, N + 2 * D, C), F32), pltpu.VMEM((N, C), F32),
        pltpu.VMEM((L, wide, C, N), BF16), dma(L, haps, 3), dma(L, haps, 3),
        opt((L, N * haps, Q), BF16), dma(L, haps, 3), dma(L, haps, 3),
        opt((L, n, rows, Q), BF16), opt((L, nz, rows, Q), BF16), dma(L, nz), dma(L, nz),
        opt((L, rows, Q), F32), opt((L, nz, rows, Q), BF16), opt((L, nz, rows, Q), BF16), dma(L, nz), dma(L, nz),
        opt((L, rows, Q), BF16), dma(L, haps), dma(L, haps),
        pltpu.VMEM((4 * L, C), F32), opt((haps, 4 * L, Cq), F32), dma(haps), dma(haps),
        opt((n, 4 * L, Cq), F32), dma(n), dma(n), opt((4 * L, Cq), F32), dma(haps), dma(haps),
    ]
    hbm = pl.BlockSpec(memory_space=pltpu.HBM)
    tg_shape = jax.ShapeDtypeStruct((N, C), BF16)
    outs = [
        tg_shape,
        jax.ShapeDtypeStruct((L, haps, rows, Q), BF16) if inside else jax.ShapeDtypeStruct((L, C, PR), F32),
        jax.ShapeDtypeStruct((haps, 4 * L, Cq) if inside else (1, 4 * L, C), F32)]
    scratch = [
        pltpu.VMEM((N, C), BF16), pltpu.VMEM((16, 128) if inside else (L, C, PR), F32), dma(2 + L)] + scratch
    params = dict(vmem_limit_bytes=60 * 1024 * 1024)
    tg, pg, sm = pl.pallas_call(
        functools.partial(kernel, n, haps, inside),
        out_shape=outs,
        in_specs=[hbm] * 6,
        out_specs=[hbm] * 3,
        scratch_shapes=scratch,
        compiler_params=pltpu.CompilerParams(collective_id=0, has_side_effects=True, **params),
    )(x, cotangent[0], gaps, jnp.transpose(conv_taps, (1, 0, 2)), norm_gains, projection)
    if inside:
        finals = [
            tg_shape, jax.ShapeDtypeStruct((L, rows, PR), F32),
            jax.ShapeDtypeStruct((3, L, C), F32), jax.ShapeDtypeStruct((L, C), F32)]
        tg, pg, taps, gains = pl.pallas_call(
            finish,
            out_shape=finals,
            in_specs=[hbm] * 3,
            out_specs=[hbm] * 4,
            scratch_shapes=[pltpu.VMEM(o.shape, o.dtype) for o in outs + finals[1:]] + [dma(2, 4)],
            compiler_params=pltpu.CompilerParams(**params),
        )(tg, pg, sm)
    else:
        pg = lax.psum(lax.psum_scatter(pg, "seq", scatter_dimension=1, tiled=True), "hap")
        sm = lax.psum(sm[0], ("seq", "hap"))
        taps, gains = sm[: 3 * L].reshape(3, L, C), sm[3 * L :]
    return tg[None], pg, jnp.transpose(taps, (1, 0, 2)), gains


def solution(mesh):
    return jax.shard_map(
        functools.partial(shards, mesh.shape["seq"], mesh.shape["hap"]),
        mesh=mesh,
        in_specs=(P("hap", "seq", None), P("hap", "seq", None), P("seq", None), P(), P(), P()),
        out_specs=(P("hap", "seq", None), P(None, "seq", None), P(), P()),
        check_vma=False,
    )
```

```python
import functools

import jax
import jax.numpy as jnp
from jax import lax
from jax.experimental import pallas as pl
from jax.experimental.pallas import tpu as pltpu
from jax.sharding import PartitionSpec as P

D = 32
LAYERS = 2
EPS = 1e-06
GELU_C = 0.7978845608028654
GELU_A = 0.044715
F32 = jnp.float32
BF16 = jnp.bfloat16
MESH = pl.DeviceIdType.MESH


def kernel(
    n, haps, inside,
    tok_hbm, cot_hbm, gaps_hbm, taps_hbm, gains_hbm, w_hbm,
    tg_hbm, pg_hbm, sm_hbm,
    tg_out, pg_out, osem, tok, cot, gaps, taps, gains, isem, w, wsem, edge_out, halo_in, hs, hr, xs, inv, npad, dgelu, hid, proj, dp, dpad, gcur,
    hT, hTs, hTr, dq_in, dqs, dqr, gbf, xr, xrs, xrr, own, zb, zr, zrs, zrr, ag, ags, agr, sml, smh, smhs, smhr, sms, smss, smsr, sma, smas, smar,
):
    me, h = lax.axis_index("seq"), lax.axis_index("hap")
    N, C = tok.shape
    PR = w.shape[2]
    Q, Cq = PR // haps, C // haps
    chunks = N // D
    outer, inner = (0, chunks - 1), tuple(range(1, chunks - 1))
    rows = C // n
    left, right = jnp.maximum(me - 1, 0), jnp.minimum(me + 1, n - 1)
    has_left, has_right = me > 0, me < n - 1
    sends = []

    loads = [pltpu.make_async_copy(w_hbm.at[l], w.at[l], wsem.at[l]) for l in range(LAYERS)]
    small_in = [
        pltpu.make_async_copy(a, b, isem.at[j])
        for j, (a, b) in enumerate(
            ((tok_hbm, tok), (gaps_hbm, gaps), (gains_hbm, gains), (taps_hbm, taps), (cot_hbm, cot)))
    ]
    for c in small_in[:4] + loads + small_in[4:]:
        c.start()

    barrier = pltpu.get_barrier_semaphore()
    if inside:
        for d in range(1, n):
            pl.semaphore_signal(barrier, inc=1, device_id={"seq": lax.rem(me + d, n)}, device_id_type=MESH)
        for d in range(1, haps):
            pl.semaphore_signal(barrier, inc=1, device_id={"hap": lax.rem(h + d, haps)}, device_id_type=MESH)
    else:
        @pl.when(has_left)
        def _():
            pl.semaphore_signal(barrier, inc=1, device_id={"seq": left}, device_id_type=MESH)

        @pl.when(has_right)
        def _():
            pl.semaphore_signal(barrier, inc=1, device_id={"seq": right}, device_id_type=MESH)

    offs = lax.broadcasted_iota(jnp.int32, (D, 1), 0)

    def valid_of(i):
        b = offs + i * D
        return jnp.where((b >= gaps[0, 0]) & (b < gaps[0, 1]), 0.0, 1.0).astype(F32)

    small_in[0].wait()
    small_in[1].wait()
    valid = [valid_of(i) for i in range(chunks)]

    def ds(i):
        return pl.ds(i * D, D)

    def at(i):
        return ds((outer + inner).index(i))

    def halo(k):
        up = pltpu.make_async_remote_copy(
            src_ref=edge_out.at[k, 1], dst_ref=halo_in.at[k, 0], send_sem=hs.at[k, 1],
            recv_sem=hr.at[k, 0], device_id={"seq": right}, device_id_type=MESH)
        down = pltpu.make_async_remote_copy(
            src_ref=edge_out.at[k, 0], dst_ref=halo_in.at[k, 1], send_sem=hs.at[k, 0],
            recv_sem=hr.at[k, 1], device_id={"seq": left}, device_id_type=MESH)
        return up, down

    def halo_start(k):
        up, down = halo(k)

        @pl.when(has_right)
        def _():
            up.start()

        @pl.when(has_left)
        def _():
            down.start()

        @pl.when(jnp.logical_not(has_left))
        def _():
            halo_in[k, 0] = jnp.zeros((D, C), BF16)

        @pl.when(jnp.logical_not(has_right))
        def _():
            halo_in[k, 1] = jnp.zeros((D, C), BF16)

    def halo_wait(k):
        up, down = halo(k)

        @pl.when(has_left)
        def _():
            up.wait_recv()

        @pl.when(has_right)
        def _():
            down.wait_recv()

    def halo_drain(k):
        up, down = halo(k)

        @pl.when(has_right)
        def _():
            up.wait_send()

        @pl.when(has_left)
        def _():
            down.wait_send()

    core = h + 1 - 2 * lax.rem(h, 2)
    peers = (h, core, lax.rem(h + 2, haps), lax.rem(core + 2, haps))

    def to_hap(src_of, dst_of, ss, rr, which=(1, 2, 3), to=None):
        out = []
        for d in which:
            t = peers[d if to is None else to]
            c = pltpu.make_async_remote_copy(
                src_ref=src_of(t), dst_ref=dst_of(d), send_sem=ss(d), recv_sem=rr(d),
                device_id={"hap": t}, device_id_type=MESH)
            c.start()
            out.append(c)
        sends.extend(out)
        return out

    def to_seq(src_of, dst_of, ss, rr):
        out = []
        for d in range(1, n):
            t = lax.rem(me + d, n)
            c = pltpu.make_async_remote_copy(
                src_ref=src_of(t), dst_ref=dst_of(d), send_sem=ss(d), recv_sem=rr(d),
                device_id={"seq": t}, device_id_type=MESH)
            c.start()
            out.append(c)
        sends.extend(out)
        return out

    xs[0] = tok[...]
    edge_out[0, 0] = (tok[ds(0), :].astype(F32) * valid[0]).astype(BF16)
    edge_out[0, 1] = (tok[ds(chunks - 1), :].astype(F32) * valid[-1]).astype(BF16)
    if inside:
        pl.semaphore_wait(barrier, n - 1 + haps - 1)
    else:
        @pl.when(has_left)
        def _():
            pl.semaphore_wait(barrier, 1)

        @pl.when(has_right)
        def _():
            pl.semaphore_wait(barrier, 1)
    halo_start(0)
    small_in[2].wait()
    small_in[3].wait()

    def rms(x):
        return lax.rsqrt(jnp.mean(x * x, axis=-1, keepdims=True) + EPS)

    def forward_chunk(l, i):
        pre = (
            taps[0, l : l + 1, :] * npad[l, ds(i), :]
            + taps[1, l : l + 1, :] * npad[l, ds(i + 1), :]
            + taps[2, l : l + 1, :] * npad[l, ds(i + 2), :]
        )
        sq = pre * pre
        th = jnp.tanh(GELU_C * (pre + GELU_A * (sq * pre)))
        half = 0.5 * (1.0 + th)
        hidden = (pre * half).astype(BF16)
        hid[l, 0, at(i), :] = hidden
        dgelu[l, ds(i), :] = half + 0.5 * pre * (1.0 - th * th) * (GELU_C * (1.0 + 3.0 * GELU_A * sq))

    hid_copies = [[[] for _ in range(4)] for _ in range(LAYERS)]

    def blocks_of(which):
        return [(0, 2 * D, N - 2 * D)] if which == inner else [(1, 0, 2 * D)]

    def send_hidden(l, which):
        if not inside:
            return
        for j, start, size in blocks_of(which):
            near, far = to_hap(
                lambda t: hid.at[l, 0, pl.ds(start, size), :], lambda d: hid.at[l, d, pl.ds(start, size), :],
                lambda d: hTs.at[l, d, j], lambda d: hTr.at[l, d, j], (1, 2))
            hid_copies[l][1].append(near)
            hid_copies[l][2].append(far)

    def relay_hidden(l):
        if inside:
            for c in hid_copies[l][2]:
                c.wait_recv()
            hid_copies[l][2] = []
            hid_copies[l][3] = to_hap(
                lambda t: hid.at[l, 2], lambda d: hid.at[l, d],
                lambda d: hTs.at[l, d, 0], lambda d: hTr.at[l, d, 0], (3,), 1)

    def turn(l, which):
        for d in which:
            if d == 0 or inside:
                for c in hid_copies[l][d]:
                    c.wait_recv()
                hT[l, d] = jnp.transpose(hid[l, d].astype(F32)).astype(BF16)

    def norm_chunk(l, i):
        v = xs[l, ds(i), :].astype(F32)
        r = rms(v)
        inv[l, ds(i), :] = r
        npad[l, ds(i + 1), :] = v * r * gains[l : l + 1, :] * valid[i]

    def project(l, which):
        y = jnp.dot(
            jnp.concatenate([hid[l, 0, at(i), :] for i in which], axis=0), w[l], preferred_element_type=F32)
        for j, i in enumerate(which):
            first = y[j * D : (j + 1) * D, 0:C]
            gate = 0.5 + 0.5 * jnp.tanh(0.5 * y[j * D : (j + 1) * D, C:PR])
            proj[l, ds(i), 0:C] = first
            proj[l, ds(i), C:PR] = gate
            if l + 1 < LAYERS:
                nxt = (xs[l, ds(i), :].astype(F32) + valid[i] * first * gate).astype(BF16)
                xs[l + 1, ds(i), :] = nxt
                if i in outer:
                    edge_out[l + 1, 0 if i == 0 else 1] = (nxt.astype(F32) * valid[i]).astype(BF16)

    def dproj(l, i):
        first = proj[l, ds(i), 0:C]
        gate = proj[l, ds(i), C:PR]
        grad = cot[ds(i), :].astype(F32) if l == LAYERS - 1 else gcur[ds(i), :]
        bg = valid[i] * grad * gate
        both = jnp.concatenate([bg, bg * first * (1.0 - gate)], axis=1).astype(BF16)
        for q in range(haps):
            dp[l, q, at(i), :] = both[:, q * Q : (q + 1) * Q]

    def send_dproj(l, which):
        if not inside:
            return
        for j, start, size in blocks_of(which):
            dq_copies[l] += to_hap(
                lambda t: dp.at[l, t, pl.ds(start, size), :],
                lambda d: dq_in.at[l, pl.ds(d * N + start, size), :],
                lambda d: dqs.at[l, d, j], lambda d: dqr.at[l, d, j])

    def dconv(l, which):
        y = lax.dot_general(
            jnp.concatenate(
                [jnp.concatenate([dp[l, q, at(i), :] for q in range(haps)], axis=1) for i in which], axis=0),
            w[l], (((1,), (1,)), ((), ())), preferred_element_type=F32)
        for j, i in enumerate(which):
            dpre = y[j * D : (j + 1) * D, :] * dgelu[l, ds(i), :]
            dpad[l, ds(i + 1), :] = dpre
            if i in outer:
                edge_out[2 * LAYERS - 1 - l, 0 if i == 0 else 1] = dpre.astype(BF16)

    def fold(v):
        return jnp.sum(v.reshape(D // 8, 8, C), axis=0)

    outs = []
    dq_copies, x_copies, z_copies, ag_copies = [[[] for _ in range(LAYERS)] for _ in range(4)]
    nz = n // 2
    z, x = me // 2, lax.rem(me, 2)
    order = [nz // 2] + [j for j in range(1, nz) if j != nz // 2] + [0]

    for l in range(LAYERS):
        last = l == LAYERS - 1
        for i in range(chunks):
            norm_chunk(l, i)
        for i in inner:
            forward_chunk(l, i)
        send_hidden(l, inner)
        loads[l].wait()
        project(l, inner)
        if last:
            small_in[4].wait()
            for i in inner:
                dproj(l, i)
            send_dproj(l, inner)
            dconv(l, inner)
        halo_wait(l)
        for side, place in ((0, 0), (1, chunks + 1)):
            v = halo_in[l, side].astype(F32)
            npad[l, ds(place), :] = v * rms(v) * gains[l : l + 1, :]
        for i in outer:
            forward_chunk(l, i)
        project(l, outer)
        if last:
            for i in outer:
                dproj(l, i)
            dconv(l, outer)
        halo_start(l + 1)
        send_hidden(l, outer)
        if last:
            send_dproj(l, outer)

    def gram(l):
        if not inside:
            pg_out[l] = jnp.dot(
                hT[l, 0], jnp.concatenate([dp[l, q] for q in range(haps)], axis=1), preferred_element_type=F32)
            return
        dq_in[l, 0:N, :] = dp[l, h]
        for c in dq_copies[l]:
            c.wait_recv()
        for j in order:
            t = lax.rem(z + j, nz)
            cut = pl.ds(pl.multiple_of(t * 2 * rows, 2 * rows), 2 * rows)
            g = jnp.dot(
                jnp.concatenate([hT[l, d, cut, :] for d in range(haps)], axis=1), dq_in[l],
                preferred_element_type=F32)
            gbf[l, pl.ds(2 * t, 2)] = g.astype(BF16).reshape(2, rows, Q)
            c = pltpu.make_async_remote_copy(
                src_ref=gbf.at[l, 2 * t + 1 - x], dst_ref=xr.at[l, j],
                send_sem=xrs.at[l, j], recv_sem=xrr.at[l, j],
                device_id={"seq": 2 * z + 1 - x}, device_id_type=MESH)
            c.start()
            x_copies[l].append(c)
        sends.extend(x_copies[l])

    def forward(l):
        for j, c in zip(order, x_copies[l]):
            t = 2 * lax.rem(z + j, nz) + x
            c.wait_recv()
            total = gbf[l, t].astype(F32) + xr[l, j].astype(F32)
            if j == 0:
                own[l] = total
                continue
            zb[l, j] = total.astype(BF16)
            c = pltpu.make_async_remote_copy(
                src_ref=zb.at[l, j], dst_ref=zr.at[l, j], send_sem=zrs.at[l, j], recv_sem=zrr.at[l, j],
                device_id={"seq": t}, device_id_type=MESH)
            c.start()
            z_copies[l].append((j, c))
            sends.append(c)

    def reduced(l):
        total = own[l]
        for j, c in z_copies[l]:
            c.wait_recv()
            total = total + zr[l, j].astype(F32)
        ag[l] = total.astype(BF16)
        ag_copies[l] = to_hap(
            lambda t: ag.at[l], lambda d: pg_hbm.at[l, h], lambda d: ags.at[l, d], lambda d: agr.at[l, d])
        c = pltpu.make_async_copy(ag.at[l], pg_hbm.at[l, h], osem.at[2 + l])
        c.start()
        outs.append(c)

    def tap_sums(l):
        t_sum = [jnp.zeros((8, C), F32) for _ in range(3)]
        for i in range(chunks):
            dpre = dpad[l, ds(i + 1), :]
            for j in range(3):
                t_sum[j] = t_sum[j] + fold(dpre * npad[l, ds(i + j), :])
        for j in range(3):
            sml[LAYERS * j + l : LAYERS * j + l + 1, :] = jnp.sum(t_sum[j], axis=0, keepdims=True)

    for l in reversed(range(LAYERS)):
        k = 2 * LAYERS - 1 - l
        last = l == LAYERS - 1
        g_sum = jnp.zeros((8, C), F32)

        def back_chunk(i, g_sum):
            dn = (
                taps[0, l : l + 1, :] * dpad[l, ds(i + 2), :]
                + taps[1, l : l + 1, :] * dpad[l, ds(i + 1), :]
                + taps[2, l : l + 1, :] * dpad[l, ds(i), :]
            )
            dq = dn * valid[i]
            v = xs[l, ds(i), :].astype(F32)
            r = inv[l, ds(i), :]
            vr = v * r
            g_sum = g_sum + fold(dq * vr)
            dt = dq * gains[l : l + 1, :]
            grad = cot[ds(i), :].astype(F32) if last else gcur[ds(i), :]
            new = grad + r * dt - vr * (r * r * jnp.mean(dt * v, axis=-1, keepdims=True))
            if l == 0:
                tg_out[ds(i), :] = new.astype(BF16)
            else:
                gcur[ds(i), :] = new
                dproj(l - 1, i)
            return g_sum

        if l == 0:
            turn(0, (3,))
            gram(0)
            for m in range(LAYERS):
                tap_sums(m)
        for i in inner:
            g_sum = back_chunk(i, g_sum)
        if l > 0:
            send_dproj(l - 1, inner)
            relay_hidden(l - 1)
            dconv(l - 1, inner)
            turn(l - 1, (0, 1, 2))
            if last:
                turn(l, (0,))
        if l == 0:
            if inside:
                for m in range(1, LAYERS):
                    forward(m)
        halo_wait(k)
        dpad[l, ds(0), :] = halo_in[k, 0].astype(F32)
        dpad[l, ds(chunks + 1), :] = halo_in[k, 1].astype(F32)
        for i in outer:
            g_sum = back_chunk(i, g_sum)
        if l > 0:
            send_dproj(l - 1, outer)
            dconv(l - 1, outer)
            halo_start(k + 1)
            if last:
                relay_hidden(l)
                turn(l, (1, 2))
            turn(l, (3,))
            gram(l)
        sml[3 * LAYERS + l : 3 * LAYERS + l + 1, :] = jnp.sum(g_sum, axis=0, keepdims=True)

    c = pltpu.make_async_copy(tg_out, tg_hbm, osem.at[0])
    c.start()
    outs.append(c)
    if inside:
        def quarter(t):
            return pl.ds(pl.multiple_of(t * Cq, Cq), Cq)

        smh[h] = sml[:, quarter(h)]
        small = to_hap(
            lambda t: sml.at[:, quarter(t)], lambda d: smh.at[h], lambda d: smhs.at[d], lambda d: smhr.at[d])
        forward(0)
        for c in small:
            c.wait_recv()
        total = smh[0]
        for q in range(1, haps):
            total = total + smh[q]
        sms[me] = total
        small = to_seq(lambda t: sms.at[me], lambda d: sms.at[me], lambda d: smss.at[d], lambda d: smsr.at[d])
        for l in range(1, LAYERS):
            reduced(l)
        reduced(0)
        for c in small:
            c.wait_recv()
        total = sms[0]
        for q in range(1, n):
            total = total + sms[q]
        sma[...] = total
        small = to_hap(lambda t: sma, lambda d: sm_hbm.at[h], lambda d: smas.at[d], lambda d: smar.at[d])
        c = pltpu.make_async_copy(sma, sm_hbm.at[h], osem.at[1])
        c.start()
        outs.append(c)
        for l in reversed(range(LAYERS)):
            small += ag_copies[l]
        for c in small:
            c.wait_recv()
    else:
        c = pltpu.make_async_copy(sml, sm_hbm.at[0], osem.at[1])
        c.start()
        outs.append(c)
        for l in range(LAYERS):
            c = pltpu.make_async_copy(pg_out.at[l], pg_hbm.at[l], osem.at[2 + l])
            c.start()
            outs.append(c)
    for k in range(2 * LAYERS):
        halo_drain(k)
    for c in sends:
        c.wait_send()
    for c in outs:
        c.wait()


def finish(tg, pg, sm, tg_hbm, pg_hbm, tp_hbm, gn_hbm, tg_v, pg_in, sm_in, pg_v, tp_v, gn_v, sem):
    L, haps, _, Q = pg.shape
    Cq = sm.shape[2]
    loads = [
        pltpu.make_async_copy(a, b, sem.at[0, j]) for j, (a, b) in enumerate(((pg, pg_in), (tg, tg_v), (sm, sm_in)))]
    stores = [
        pltpu.make_async_copy(a, b, sem.at[1, j])
        for j, (a, b) in enumerate(((pg_v, pg_hbm), (tg_v, tg_hbm), (tp_v, tp_hbm), (gn_v, gn_hbm)))]
    for c in loads:
        c.start()
    loads[0].wait()
    for l in range(L):
        for q in range(haps):
            pg_v[l, :, q * Q : (q + 1) * Q] = pg_in[l, q].astype(F32)
    stores[0].start()
    loads[1].wait()
    stores[1].start()
    loads[2].wait()
    for q in range(haps):
        for j in range(3):
            tp_v[j, :, q * Cq : (q + 1) * Cq] = sm_in[q, j * L : (j + 1) * L, :]
        gn_v[:, q * Cq : (q + 1) * Cq] = sm_in[q, 3 * L :, :]
    stores[2].start()
    stores[3].start()
    for c in stores:
        c.wait()


def shards(n, haps, tokens, cotangent, gaps, conv_taps, norm_gains, projection):
    x = tokens[0]
    N, C = x.shape
    PR = projection.shape[2]
    inside = n > 2 and n % 2 == 0 and haps == 4 and C % (16 * n) == 0 and C % (128 * haps) == 0
    Cq, nz = C // haps, max(n // 2, 1)
    Q, rows = PR // haps, max(C // n, 1)
    L = LAYERS
    wide = haps if inside else 1

    def dma(*shape):
        return pltpu.SemaphoreType.DMA(shape)

    def opt(shape, dtype):
        return pltpu.VMEM(shape if inside else (16, 128), dtype)

    scratch = [
        pltpu.VMEM((N, C), BF16), pltpu.VMEM((N, C), BF16), pltpu.SMEM(gaps.shape, jnp.int32),
        pltpu.VMEM((3, L, C), F32), pltpu.VMEM((L, C), F32), dma(5),
        pltpu.VMEM((L, C, PR), BF16), dma(L),
        pltpu.VMEM((2 * L, 2, D, C), BF16), pltpu.VMEM((2 * L, 2, D, C), BF16), dma(2 * L, 2), dma(2 * L, 2),
        pltpu.VMEM((L, N, C), BF16), pltpu.VMEM((L, N, 1), F32), pltpu.VMEM((L, N + 2 * D, C), F32),
        pltpu.VMEM((L, N, C), F32), pltpu.VMEM((L, wide, N, C), BF16), pltpu.VMEM((L, N, PR), F32),
        pltpu.VMEM((L, haps, N, Q), BF16), pltpu.VMEM((L, N + 2 * D, C), F32), pltpu.VMEM((N, C), F32),
        pltpu.VMEM((L, wide, C, N), BF16), dma(L, haps, 3), dma(L, haps, 3),
        opt((L, N * haps, Q), BF16), dma(L, haps, 3), dma(L, haps, 3),
        opt((L, n, rows, Q), BF16), opt((L, nz, rows, Q), BF16), dma(L, nz), dma(L, nz),
        opt((L, rows, Q), F32), opt((L, nz, rows, Q), BF16), opt((L, nz, rows, Q), BF16), dma(L, nz), dma(L, nz),
        opt((L, rows, Q), BF16), dma(L, haps), dma(L, haps),
        pltpu.VMEM((4 * L, C), F32), opt((haps, 4 * L, Cq), F32), dma(haps), dma(haps),
        opt((n, 4 * L, Cq), F32), dma(n), dma(n), opt((4 * L, Cq), F32), dma(haps), dma(haps),
    ]
    hbm = pl.BlockSpec(memory_space=pltpu.HBM)
    tg_shape = jax.ShapeDtypeStruct((N, C), BF16)
    outs = [
        tg_shape,
        jax.ShapeDtypeStruct((L, haps, rows, Q), BF16) if inside else jax.ShapeDtypeStruct((L, C, PR), F32),
        jax.ShapeDtypeStruct((haps, 4 * L, Cq) if inside else (1, 4 * L, C), F32)]
    scratch = [
        pltpu.VMEM((N, C), BF16), pltpu.VMEM((16, 128) if inside else (L, C, PR), F32), dma(2 + L)] + scratch
    params = dict(vmem_limit_bytes=60 * 1024 * 1024)
    tg, pg, sm = pl.pallas_call(
        functools.partial(kernel, n, haps, inside),
        out_shape=outs,
        in_specs=[hbm] * 6,
        out_specs=[hbm] * 3,
        scratch_shapes=scratch,
        compiler_params=pltpu.CompilerParams(collective_id=0, has_side_effects=True, **params),
    )(x, cotangent[0], gaps, jnp.transpose(conv_taps, (1, 0, 2)), norm_gains, projection)
    if inside:
        finals = [
            tg_shape, jax.ShapeDtypeStruct((L, rows, PR), F32),
            jax.ShapeDtypeStruct((3, L, C), F32), jax.ShapeDtypeStruct((L, C), F32)]
        tg, pg, taps, gains = pl.pallas_call(
            finish,
            out_shape=finals,
            in_specs=[hbm] * 3,
            out_specs=[hbm] * 4,
            scratch_shapes=[pltpu.VMEM(o.shape, o.dtype) for o in outs + finals[1:]] + [dma(2, 4)],
            compiler_params=pltpu.CompilerParams(**params),
        )(tg, pg, sm)
    else:
        pg = lax.psum(lax.psum_scatter(pg, "seq", scatter_dimension=1, tiled=True), "hap")
        sm = lax.psum(sm[0], ("seq", "hap"))
        taps, gains = sm[: 3 * L].reshape(3, L, C), sm[3 * L :]
    return tg[None], pg, jnp.transpose(taps, (1, 0, 2)), gains


def solution(mesh):
    return jax.shard_map(
        functools.partial(shards, mesh.shape["seq"], mesh.shape["hap"]),
        mesh=mesh,
        in_specs=(P("hap", "seq", None), P("hap", "seq", None), P("seq", None), P(), P(), P()),
        out_specs=(P("hap", "seq", None), P(None, "seq", None), P(), P()),
        check_vma=False,
    )
```
